32 devices in a mesh: vocab: 8 (over z, x), dp: 4 (over y, core).
Axes of the slice: x: 2, y: 2, z: 4, core: 2. Of those that a mesh axis runs over, the one named last changes fastest.
Arguments:
- hidden: bfloat16 [1024, 8192], P('dp', 'vocab'), may hold values from -49.67767 to 49.67767
- targets: int32 [1024], P('dp'), may hold values from 0 to 2047
- loss_mask: int32 [1024], P('dp'), may hold values from 0 to 1, as said below
- master: float32 [2048, 8192], P(('vocab', 'dp')), may hold values from -1 to 1
- first_moment: float32 [2048, 8192], P(('vocab', 'dp')), may hold values from -0.00390625 to 0.00390625
- second_moment: float32 [2048, 8192], P(('vocab', 'dp')), may hold values from 1.4901161e-08 to 2.3841858e-07
Outputs:
- loss_value: float32 [], replicated
- hidden_grad: bfloat16 [1024, 8192], P('dp', 'vocab')
- new_master: float32 [2048, 8192], P(('vocab', 'dp'))
- new_first: float32 [2048, 8192], P(('vocab', 'dp'))
- new_second: float32 [2048, 8192], P(('vocab', 'dp'))
The draws below stay inside these ranges and needn't reach their ends.
Inputs may be any that keep to these rules, and one draw needn't show every extreme that they name: `loss_mask`: the first position of every aligned block of 256 positions is 1.
All inputs are finite; a program needn't handle non-finite values.
Results may differ from the reference program's by a relative error of at most 0.02.
Values may be sent and summed in bfloat16 or wider, within the bound.
A program may use at most 128 MiB of HBM per device.

```python
import math
import jax
import jax.numpy as jnp
import numpy as np
from jax import lax

D = 8192
TOK_DEV = 256
STEP = 10
V_DEV = 256
VOCAB = 2048
TOKENS = 1024
N_VOCAB = 8
N_DP = 4


def single_row(base_key, row_index):
    return jax.random.truncated_normal(jax.random.fold_in(base_key, row_index), -4.0, 4.0, (D,), jnp.float32) / math.sqrt(D)


def head_table(key):
    base_key = jax.random.fold_in(key, 17)
    return jax.vmap(lambda row_index: single_row(base_key, row_index))(jnp.arange(VOCAB))


def draw_master(key, part):
    return head_table(key)


def draw_hidden(key, part):
    noise = 3.0 * jax.random.truncated_normal(jax.random.fold_in(key, 5), -3.5, 3.5, (TOKENS, D), jnp.float32)
    return noise.astype(jnp.bfloat16)


def draw_loss_mask(key, part):
    positions = jnp.arange(TOKENS)
    blocks_total = TOKENS // TOK_DEV
    block_index = positions // TOK_DEV
    limit = 30 + 60 * block_index // max(blocks_total - 1, 1)
    rolls = jax.random.randint(jax.random.fold_in(key, 23), (TOKENS,), 0, 100)
    valid = (rolls < limit) | (positions % TOK_DEV == 0)
    return valid.astype(jnp.int32)


def set_ends(values, stream_key, low, largest):
    index_at = [jax.random.randint(jax.random.fold_in(stream_key, axis), (), 0, length) for axis, length in enumerate(values.shape)]
    widest = values.shape.index(max(values.shape))
    next_to = index_at[:widest] + [(index_at[widest] + 1) % values.shape[widest]] + index_at[widest + 1:]
    return values.at[tuple(index_at)].set(low).at[tuple(next_to)].set(largest)


def levels(key, shape, cuts, least, largest):
    def one(dim, shards_of):
        heights = jax.random.uniform(jax.random.fold_in(jax.random.fold_in(key, 6), dim), (shards_of,), jnp.float32, least / len(cuts), largest / len(cuts))
        return jnp.repeat(jnp.exp(heights), shape[dim] // shards_of).reshape((-1,) + (1,) * (len(shape) - dim - 1))

    factor_of = one(*cuts[0])
    for cut in cuts[1:]:
        factor_of = factor_of * one(*cut)
    return factor_of


def rank_bounds(count, lean):
    loads = [(1 << 20) // math.isqrt(standing ** lean) + 1 for standing in range(1, count + 1)]
    deviation = 1 + sum(loads) // (1 << 30)
    return np.cumsum(np.array([max(1, weight // deviation) for weight in loads]))


def ranked_ids(stream_key, dims, amount, slope):
    grid = rank_bounds(amount, slope)
    lot = jax.random.randint(jax.random.fold_in(stream_key, 1), dims, 0, int(grid[amount - 1]))
    rank = jnp.searchsorted(jnp.asarray(grid, jnp.int32), lot, side="right")
    return jax.random.permutation(jax.random.fold_in(stream_key, 2), amount)[rank].astype(jnp.int32)


def scatter_about(own_key, extent, width, most, cuts=(), dtype=jnp.bfloat16):
    entries = width * jax.random.normal(own_key, extent, jnp.float32)
    if cuts:
        entries = entries * levels(own_key, extent, cuts, -0.22, 0.18)
    return jnp.clip(entries, -most, most).astype(dtype)


def setup_inputs(seed: int = 0) -> dict:
    key_of = jax.random.split(jax.random.key(seed), 7)
    hidden = draw_hidden(jax.random.fold_in(key_of[6], 71), 0)
    targets = set_ends(ranked_ids(key_of[1], (TOKENS,), VOCAB, 2), jax.random.fold_in(key_of[1], 3), 0, VOCAB - 1).astype(jnp.int32)
    loss_mask = draw_loss_mask(jax.random.fold_in(key_of[6], 71), 0)
    master = draw_master(jax.random.fold_in(key_of[6], 71), 0)
    first_moment = scatter_about(key_of[4], (VOCAB, D), ((VOCAB * D) ** -0.5), 0.00390625, ((0, 32),), jnp.float32)
    second_moment = jnp.clip(jnp.exp(math.log(2.384185791015625e-07) - 2.7725887 * jax.random.uniform(key_of[5], (VOCAB, D), jnp.float32) ** levels(key_of[5], (VOCAB, D), ((0, 32),), -0.2, 0.2)), 1.4901161193847656e-08, 2.384185791015625e-07)
    return {"hidden": hidden, "targets": targets, "loss_mask": loss_mask, "master": master, "first_moment": first_moment, "second_moment": second_moment}


beta_one = 0.9
beta_two = 0.95
learn_rate = 0.0003
decay_rate = 0.1
epsilon_adam = 1e-08
clip_norm = 1.0

def reference(hidden, targets, loss_mask, master, first_moment, second_moment):
    weights_half = master.astype(jnp.bfloat16)
    logits = jnp.dot(hidden, weights_half.T, preferred_element_type=jnp.float32)
    row_top = lax.optimization_barrier(jnp.max(logits, axis=1))
    exp_sum = lax.optimization_barrier(jnp.sum(jnp.exp(logits - row_top[:, None]), axis=1))
    log_norm = row_top + jnp.log(exp_sum)
    columns = lax.broadcasted_iota(jnp.int32, (1, VOCAB), 1)
    onehot = (columns == targets[:, None]).astype(jnp.float32)
    picked = lax.optimization_barrier(jnp.sum(onehot * logits, axis=1))
    mask_float = loss_mask.astype(jnp.float32)
    valid_count = jnp.sum(mask_float)
    loss_value = jnp.sum(mask_float * (log_norm - picked)) / valid_count
    logit_grad = (mask_float[:, None] * (jnp.exp(logits - log_norm[:, None]) - onehot)).astype(jnp.bfloat16)

    def add_block(running, pieces):
        grad_block, head_block = pieces
        block_term = jnp.dot(grad_block, head_block, preferred_element_type=jnp.float32)
        rounded = lax.optimization_barrier(block_term.astype(jnp.bfloat16))
        return (running + rounded.astype(jnp.float32), None)
    grad_blocks = jnp.transpose(logit_grad.reshape(TOKENS, N_VOCAB, V_DEV), (1, 0, 2))
    head_blocks = weights_half.reshape(N_VOCAB, V_DEV, D)
    hidden_term, unused_one = lax.scan(add_block, jnp.zeros((TOKENS, D), jnp.float32), (grad_blocks, head_blocks))
    hidden_grad = (hidden_term / valid_count).astype(jnp.bfloat16)

    def accumulate(running, pieces):
        grad_rows, hidden_rows = pieces
        partial_term = jnp.dot(grad_rows.T, hidden_rows, preferred_element_type=jnp.float32)
        rounded = lax.optimization_barrier(partial_term.astype(jnp.bfloat16))
        return (running + rounded.astype(jnp.float32), None)
    grad_groups = logit_grad.reshape(N_DP, TOK_DEV, VOCAB)
    hidden_groups = hidden.reshape(N_DP, TOK_DEV, D)
    weight_raw, unused_two = lax.scan(accumulate, jnp.zeros((VOCAB, D), jnp.float32), (grad_groups, hidden_groups))
    weight_grad = weight_raw / valid_count
    grad_norm = jnp.sqrt(jnp.sum(weight_grad * weight_grad))
    clip_factor = jnp.minimum(1.0, clip_norm / (grad_norm + 1e-06))
    clipped = weight_grad * clip_factor
    new_first = beta_one * first_moment + (1.0 - beta_one) * clipped
    new_second = beta_two * second_moment + (1.0 - beta_two) * clipped * clipped
    first_bias = 1.0 - beta_one ** STEP
    second_bias = 1.0 - beta_two ** STEP
    update = new_first / first_bias / (jnp.sqrt(new_second / second_bias) + epsilon_adam) + decay_rate * master
    new_master = master - learn_rate * update
    return (loss_value, hidden_grad, new_master, new_first, new_second)
```

```python
import functools

import jax
import jax.numpy as jnp
from jax import lax
from jax.experimental import pallas as pl
from jax.experimental.pallas import tpu as pltpu
from jax.sharding import PartitionSpec as P

STEP = 10

beta_one = 0.9
beta_two = 0.95
learn_rate = 0.0003
decay_rate = 0.1
epsilon_adam = 1e-08
clip_norm = 1.0

MESH = pl.DeviceIdType.MESH
F32 = jnp.float32
BF16 = jnp.bfloat16


def kernel(
    n_vocab, n_dp,
    hid, master, targets, mask,
    hgrad_out, wgrad_out, scal_out,
    Wg, wsend, Hg, acc, lrecv, gt, gtp,
    htsend, htrecv, gsend, grecv, gown, ysend, yrecv, xsend, xrecv,
    stat, cnt, sqa, sqb,
    z_send, z_recv, wx_send, wy_send, ws_send, w_recv,
    l_send, l_recv, st_send, st_recv, ht_send, ht_recv,
    g_send, g_recv, y_send, y_recv, x_send, x_recv,
    c_send, c_recv, a_send, a_recv, b_send, b_recv,
):
    n_o = n_vocab // 2
    n_y = n_dp // 2
    v = lax.axis_index("vocab")
    r = lax.axis_index("dp")
    o = v // 2
    i = v % 2
    y = r // 2
    c = r % 2
    rows = master.shape[0]
    blk = hid.shape[1]
    toks = hid.shape[0]
    group = 2 * n_dp * rows
    x_peer = (o * 2 + 1 - i, r)
    sibling = (v, y * 2 + 1 - c)

    def y_at(dy):
        return lax.rem(y + dy, n_y)

    def y_peer(dy):
        return (v, y_at(dy) * 2 + c)

    def rcopy(src, dst, ssem, rsem, dev):
        return pltpu.make_async_remote_copy(
            src_ref=src, dst_ref=dst, send_sem=ssem, recv_sem=rsem,
            device_id=dev, device_id_type=MESH,
        )

    barrier = pltpu.get_barrier_semaphore()
    for k in range(1, n_vocab):
        pl.semaphore_signal(barrier, inc=1, device_id=(lax.rem(v + k, n_vocab), r), device_id_type=MESH)
    for k in range(1, n_dp):
        pl.semaphore_signal(barrier, inc=1, device_id=(v, lax.rem(r + k, n_dp)), device_id_type=MESH)
    pl.semaphore_wait(barrier, n_vocab - 1 + n_dp - 1)

    sends = []

    def z_copy(src, b, side):
        peer = o + 1 if side == 0 else o - 1
        return rcopy(src, Hg.at[b], z_send.at[side, b], z_recv.at[b], (peer * 2 + i, r))

    @pl.when(o < n_o - 1)
    def _():
        z_copy(hid, o, 0).start()

    @pl.when(o > 0)
    def _():
        z_copy(hid, o, 1).start()

    def z_step(d, then):
        @pl.when(o - d >= 0)
        def _():
            b = o - d
            z_copy(hid, b, 0).wait_recv()

            @pl.when(o < n_o - 1)
            def _():
                z_copy(Hg.at[b], b, 0).start()

            then(b)

        @pl.when(o + d < n_o)
        def _():
            b = o + d
            z_copy(hid, b, 1).wait_recv()

            @pl.when(o > 0)
            def _():
                z_copy(Hg.at[b], b, 1).start()

            then(b)

    def slot(ii, rr):
        return pl.ds(pl.multiple_of((ii * n_dp + rr) * rows, rows), rows)

    def w_slot(ii, rr):
        return Wg.at[:, slot(ii, rr), :]

    def w_sem(ii, rr):
        return w_recv.at[ii * n_dp + rr]

    def w_y(dy, k, ii):
        return rcopy(w_slot(ii, r), w_slot(ii, r), wy_send.at[dy - 1, k], w_sem(ii, r), y_peer(dy))

    def w_s(dy, k, ii):
        rr = y_at(dy) * 2 + c
        return rcopy(w_slot(ii, rr), w_slot(ii, rr), ws_send.at[dy, k], w_sem(ii, rr), sibling)

    def w_wait(ii, rr):
        rcopy(w_slot(ii, rr), w_slot(ii, rr), wx_send.at[0], w_sem(ii, rr), x_peer).wait_recv()

    for b in range(n_o):
        cols = pl.ds(pl.multiple_of((2 * b + 1 - i) * blk, blk), blk)
        wsend[b] = master[:, cols].astype(BF16)
    wx = rcopy(wsend, w_slot(i, r), wx_send.at[0], w_sem(i, r), x_peer)
    wx.start()
    sends.append(wx)
    for b in range(n_o):
        cols = pl.ds(pl.multiple_of((2 * b + i) * blk, blk), blk)
        Wg[b, slot(i, r), :] = master[:, cols].astype(BF16)
    for dy in range(1, n_y):
        q = w_y(dy, 0, i)
        q.start()
        sends.append(q)
    q = w_s(0, 0, i)
    q.start()
    sends.append(q)

    maskf = mask[...].astype(F32)
    cnt[r] = jnp.broadcast_to(jnp.sum(maskf, axis=1, keepdims=True), cnt.shape[1:])
    for k in range(1, n_dp):
        q = rcopy(cnt.at[r], cnt.at[r], c_send.at[k], c_recv.at[r], (v, lax.rem(r + k, n_dp)))
        q.start()
        sends.append(q)
    Hg[o] = hid[...]
    acc[...] = jnp.zeros_like(acc)

    def nothing(b):
        return None

    w_wait(1 - i, r)
    for dy in range(1, n_y):
        q = w_y(dy, 1, 1 - i)
        q.start()
        sends.append(q)
    q = w_s(0, 1, 1 - i)
    q.start()
    sends.append(q)
    z_step(1, nothing)
    for dy in range(1, n_y):
        w_wait(i, y_at(dy) * 2 + c)
        q = w_s(dy, 0, i)
        q.start()
        sends.append(q)
    if n_o > 2:
        z_step(2, nothing)
    for dy in range(1, n_y):
        w_wait(1 - i, y_at(dy) * 2 + c)
        q = w_s(dy, 1, 1 - i)
        q.start()
        sends.append(q)
    for dy in range(n_y):
        for ii in range(2):
            w_wait(ii, y_at(dy) * 2 + 1 - c)

    def logits_of(b):
        acc[...] += lax.dot_general(
            Wg[b], Hg[b], (((1,), (1,)), ((), ())), preferred_element_type=F32
        )

    logits_of(o)
    for d in range(1, min(n_o, 3)):
        @pl.when(o - d >= 0)
        def _():
            logits_of(o - d)

        @pl.when(o + d < n_o)
        def _():
            logits_of(o + d)
    for d in range(3, n_o):
        z_step(d, logits_of)

    q = rcopy(acc, lrecv, l_send.at[0], l_recv.at[0], x_peer)
    q.start()
    q.wait()
    acc[...] = acc[...] + lrecv[...]

    logits = acc[...]
    ids = targets[...] - o * group
    onehot = (lax.broadcasted_iota(jnp.int32, (group, toks), 0) == ids).astype(F32)
    top = jnp.max(logits, axis=0, keepdims=True)
    stat[o] = jnp.zeros(stat.shape[1:], F32)
    stat[o, 0:1, :] = top
    stat[o, 1:2, :] = jnp.sum(jnp.exp(logits - top), axis=0, keepdims=True)
    stat[o, 2:3, :] = jnp.sum(onehot * logits, axis=0, keepdims=True)
    st = []
    for k in range(1, n_o):
        q = rcopy(stat.at[o], stat.at[o], st_send.at[k], st_recv.at[o], (lax.rem(o + k, n_o) * 2 + i, r))
        q.start()
        sends.append(q)
    for k in range(1, n_o):
        b = lax.rem(o + k, n_o)
        rcopy(stat.at[b], stat.at[b], st_send.at[k], st_recv.at[b], x_peer).wait_recv()
    row_top = stat[0, 0:1, :]
    for b in range(1, n_o):
        row_top = jnp.maximum(row_top, stat[b, 0:1, :])
    exp_sum = jnp.zeros_like(row_top)
    picked = jnp.zeros_like(row_top)
    for b in range(n_o):
        exp_sum += stat[b, 1:2, :] * jnp.exp(stat[b, 0:1, :] - row_top)
        picked += stat[b, 2:3, :]
    log_norm = row_top + jnp.log(exp_sum)
    loss_local = jnp.sum(maskf * (log_norm - picked), axis=1, keepdims=True)
    grad = maskf * (jnp.exp(acc[...] - log_norm) - onehot)
    gt[...] = grad.astype(BF16)

    g_tv = grad.T.astype(BF16)
    half = n_o // 2
    order = []
    for k in range(1, n_o):
        order.append(half + (k // 2) * (1 if k % 2 else -1))
    order = [k for k in order if 0 < k < n_o]
    for k in range(1, n_o):
        if k not in order:
            order.append(k)
    for k in order:
        b = lax.rem(o + k, n_o)
        htsend[k - 1] = jnp.dot(g_tv, Wg[b], preferred_element_type=F32).astype(BF16)
        q = rcopy(htsend.at[k - 1], htrecv.at[k - 1], ht_send.at[k - 1], ht_recv.at[k - 1], (b * 2 + i, r))
        q.start()
        sends.append(q)

    m = 0
    for cc in (1 - c, c):
        for dy in list(range(1, n_y)) + [0]:
            for ii in (1 - i, i):
                gtp[m * rows:(m + 1) * rows, :] = gt[slot(ii, y_at(dy) * 2 + cc), :]
                m += 1
    mid = group // 2
    for b in range(n_o):
        gsend[b] = jnp.dot(gtp[:mid, :], Hg[b], preferred_element_type=F32).astype(BF16)
        q = rcopy(gsend.at[b], grecv.at[b], g_send.at[b], g_recv.at[b], sibling)
        q.start()
        sends.append(q)
    for b in range(n_o):
        gown[b] = jnp.dot(gtp[mid:, :], Hg[b], preferred_element_type=F32)
    for b in range(n_o):
        rcopy(gsend.at[b], grecv.at[b], g_send.at[b], g_recv.at[b], sibling).wait_recv()
        for dy in range(1, n_y):
            part = slice((dy - 1) * 2 * rows, dy * 2 * rows)
            ysend[dy - 1, b] = (gown[b, part, :] + grecv[b, part, :].astype(F32)).astype(BF16)
            q = rcopy(
                ysend.at[dy - 1, b], yrecv.at[dy - 1, b], y_send.at[dy - 1, b], y_recv.at[dy - 1, b], y_peer(dy)
            )
            q.start()
            sends.append(q)
    htown = jnp.dot(g_tv, Wg[o], preferred_element_type=F32)
    last = slice((n_y - 1) * 2 * rows, n_y * 2 * rows)
    squares = jnp.zeros((8, blk), F32)
    for b in range(n_o):
        total = gown[b, last, :] + grecv[b, last, :].astype(F32)
        for dy in range(1, n_y):
            rcopy(
                ysend.at[dy - 1, b], yrecv.at[dy - 1, b], y_send.at[dy - 1, b], y_recv.at[dy - 1, b], y_peer(dy)
            ).wait_recv()
            total += yrecv[dy - 1, b].astype(F32)
        xsend[b] = total[:rows].astype(BF16)
        q = rcopy(xsend.at[b], xrecv.at[b], x_send.at[b], x_recv.at[b], x_peer)
        q.start()
        sends.append(q)
        mine = total[rows:]
        wgrad_out[:, pl.ds(pl.multiple_of((2 * b + i) * blk, blk), blk)] = mine
        squares += jnp.sum((mine * mine).reshape(rows // 8, 8, blk), axis=0)
    for b in range(n_o):
        rcopy(xsend.at[b], xrecv.at[b], x_send.at[b], x_recv.at[b], x_peer).wait_recv()
        theirs = xrecv[b].astype(F32)
        wgrad_out[:, pl.ds(pl.multiple_of((2 * b + 1 - i) * blk, blk), blk)] = theirs
        squares += jnp.sum((theirs * theirs).reshape(rows // 8, 8, blk), axis=0)
    square = jnp.sum(jnp.sum(squares, axis=0, keepdims=True), axis=1, keepdims=True)

    sqa[r, 0:8, :] = jnp.broadcast_to(square, (8, 128))
    sqa[r, 8:16, :] = jnp.broadcast_to(loss_local, (8, 128))
    for k in range(1, n_dp):
        q = rcopy(sqa.at[r], sqa.at[r], a_send.at[k], a_recv.at[r], (v, lax.rem(r + k, n_dp)))
        q.start()
        sends.append(q)
    for k in range(1, n_dp):
        b = lax.rem(r + k, n_dp)
        rcopy(sqa.at[b], sqa.at[b], a_send.at[k], a_recv.at[b], x_peer).wait_recv()
        rcopy(cnt.at[b], cnt.at[b], c_send.at[k], c_recv.at[b], x_peer).wait_recv()
    both = sqa[0]
    count = cnt[0]
    for b in range(1, n_dp):
        both = both + sqa[b]
        count = count + cnt[b]
    sqb[v] = both[0:8]
    for k in range(1, n_vocab):
        q = rcopy(sqb.at[v], sqb.at[v], b_send.at[k], b_recv.at[v], (lax.rem(v + k, n_vocab), r))
        q.start()
        sends.append(q)

    for k in range(1, n_o):
        rcopy(htsend.at[k - 1], htrecv.at[k - 1], ht_send.at[k - 1], ht_recv.at[k - 1], x_peer).wait_recv()
        htown += htrecv[k - 1].astype(F32)
    hgrad_out[...] = (htown / count[0:1, 0:1]).astype(BF16)

    for k in range(1, n_vocab):
        b = lax.rem(v + k, n_vocab)
        rcopy(sqb.at[b], sqb.at[b], b_send.at[k], b_recv.at[b], x_peer).wait_recv()
    square_sum = sqb[0]
    for b in range(1, n_vocab):
        square_sum = square_sum + sqb[b]
    scal_out[0:8, :] = square_sum
    scal_out[8:16, :] = both[8:16]
    scal_out[16:24, :] = count

    for q in sends:
        q.wait_send()

    @pl.when(o < n_o - 1)
    def _():
        z_copy(hid, o, 0).wait_send()

    @pl.when(o > 0)
    def _():
        z_copy(hid, o, 1).wait_send()

    for d in range(1, n_o):
        @pl.when((o - d >= 0) & (o < n_o - 1))
        def _():
            z_copy(hid, o - d, 0).wait_send()

        @pl.when((o + d < n_o) & (o > 0))
        def _():
            z_copy(hid, o + d, 1).wait_send()


def on_device(hidden, targets, loss_mask, master, first_moment, second_moment):
    n_vocab, n_dp = lax.axis_size("vocab"), lax.axis_size("dp")
    n_o, n_y = n_vocab // 2, n_dp // 2
    toks, blk = hidden.shape
    rows, feats = master.shape
    group = 2 * n_dp * rows
    mid = group // 2
    vmem = pl.BlockSpec(memory_space=pltpu.VMEM)
    dma = pltpu.SemaphoreType.DMA
    hidden_grad, weight_raw, scal = pl.pallas_call(
        functools.partial(kernel, n_vocab, n_dp),
        out_shape=(
            jax.ShapeDtypeStruct((toks, blk), BF16),
            jax.ShapeDtypeStruct((rows, feats), F32),
            jax.ShapeDtypeStruct((24, 128), F32),
        ),
        in_specs=[vmem] * 4,
        out_specs=(vmem, vmem, vmem),
        scratch_shapes=[
            pltpu.VMEM((n_o, group, blk), BF16),
            pltpu.VMEM((n_o, rows, blk), BF16),
            pltpu.VMEM((n_o, toks, blk), BF16),
            pltpu.VMEM((group, toks), F32),
            pltpu.VMEM((group, toks), F32),
            pltpu.VMEM((group, toks), BF16),
            pltpu.VMEM((group, toks), BF16),
            pltpu.VMEM((n_o - 1, toks, blk), BF16),
            pltpu.VMEM((n_o - 1, toks, blk), BF16),
            pltpu.VMEM((n_o, mid, blk), BF16),
            pltpu.VMEM((n_o, mid, blk), BF16),
            pltpu.VMEM((n_o, mid, blk), F32),
            pltpu.VMEM((n_y - 1, n_o, 2 * rows, blk), BF16),
            pltpu.VMEM((n_y - 1, n_o, 2 * rows, blk), BF16),
            pltpu.VMEM((n_o, rows, blk), BF16),
            pltpu.VMEM((n_o, rows, blk), BF16),
            pltpu.VMEM((n_o, 8, toks), F32),
            pltpu.VMEM((n_dp, 8, 128), F32),
            pltpu.VMEM((n_dp, 16, 128), F32),
            pltpu.VMEM((n_vocab, 8, 128), F32),
            dma((2, n_o)), dma((n_o,)),
            dma((1,)), dma((n_y - 1, 2)), dma((n_y, 2)), dma((2 * n_dp,)),
            dma((1,)), dma((1,)),
            dma((n_o,)), dma((n_o,)),
            dma((n_o - 1,)), dma((n_o - 1,)),
            dma((n_o,)), dma((n_o,)),
            dma((n_y - 1, n_o)), dma((n_y - 1, n_o)),
            dma((n_o,)), dma((n_o,)),
            dma((n_dp,)), dma((n_dp,)),
            dma((n_dp,)), dma((n_dp,)),
            dma((n_vocab,)), dma((n_vocab,)),
        ],
        compiler_params=pltpu.CompilerParams(
            collective_id=0, has_side_effects=True, vmem_limit_bytes=60 * 1024 * 1024
        ),
        name="head",
    )(hidden, master, targets.reshape(1, toks), loss_mask.reshape(1, toks))
    square_sum, loss_sum, valid_count = scal[0, 0], scal[8, 0], scal[16, 0]
    loss_value = loss_sum / valid_count
    grad_norm = jnp.sqrt(square_sum) / valid_count
    clip_factor = jnp.minimum(1.0, clip_norm / (grad_norm + 1e-06))
    clipped = weight_raw / valid_count * clip_factor
    new_first = beta_one * first_moment + (1.0 - beta_one) * clipped
    new_second = beta_two * second_moment + (1.0 - beta_two) * clipped * clipped
    first_bias = 1.0 - beta_one**STEP
    second_bias = 1.0 - beta_two**STEP
    update = (
        new_first / first_bias / (jnp.sqrt(new_second / second_bias) + epsilon_adam)
        + decay_rate * master
    )
    new_master = master - learn_rate * update
    return (loss_value, hidden_grad, new_master, new_first, new_second)


def solution(mesh):
    placed = (
        P("dp", "vocab"),
        P("dp"),
        P("dp"),
        P(("vocab", "dp"), None),
        P(("vocab", "dp"), None),
        P(("vocab", "dp"), None),
    )
    return jax.shard_map(
        on_device,
        mesh=mesh,
        in_specs=placed,
        out_specs=(
            P(),
            P("dp", "vocab"),
            P(("vocab", "dp"), None),
            P(("vocab", "dp"), None),
            P(("vocab", "dp"), None),
        ),
        check_vma=False,
    )
```

```python
import functools
import math

import jax
import jax.numpy as jnp
from jax import lax
from jax.experimental import pallas as pl
from jax.experimental.pallas import tpu as pltpu
from jax.sharding import PartitionSpec as P

STEP = 10

beta_one = 0.9
beta_two = 0.95
learn_rate = 0.0003
decay_rate = 0.1
epsilon_adam = 1e-08
clip_norm = 1.0

MESH = pl.DeviceIdType.MESH
F32 = jnp.float32
BF16 = jnp.bfloat16


def kernel(
    n_vocab, n_dp,
    hid, master, targets, mask,
    hgrad_out, wgrad_out, scal_out,
    Wg, wsend, Hg, acc, lrecv, gt, gtp, g_tv,
    htsend, htrecv, gsend, grecv, gown, ysend, yrecv, xsend, xrecv,
    stat, cnt, sqa, sqb,
    z_send, z_recv, wx_send, wy_send, ws_send, w_recv,
    l_send, l_recv, st_send, st_recv, ht_send, ht_recv,
    g_send, g_recv, y_send, y_recv, x_send, x_recv,
    c_send, c_recv, a_send, a_recv, b_send, b_recv,
):
    n_o = n_vocab // 2
    n_y = n_dp // 2
    v = lax.axis_index("vocab")
    r = lax.axis_index("dp")
    o = v // 2
    i = v % 2
    y = r // 2
    c = r % 2
    rows = master.shape[0]
    blk = hid.shape[1]
    toks = hid.shape[0]
    group = 2 * n_dp * rows
    th = toks // 2
    x_peer = (o * 2 + 1 - i, r)
    sibling = (v, y * 2 + 1 - c)

    def y_at(dy):
        return lax.rem(y + dy, n_y)

    def y_peer(dy):
        return (v, y_at(dy) * 2 + c)

    def rcopy(src, dst, ssem, rsem, dev):
        return pltpu.make_async_remote_copy(
            src_ref=src, dst_ref=dst, send_sem=ssem, recv_sem=rsem,
            device_id=dev, device_id_type=MESH,
        )

    barrier = pltpu.get_barrier_semaphore()
    for k in range(1, n_vocab):
        pl.semaphore_signal(barrier, inc=1, device_id=(lax.rem(v + k, n_vocab), r), device_id_type=MESH)
    for k in range(1, n_dp):
        pl.semaphore_signal(barrier, inc=1, device_id=(v, lax.rem(r + k, n_dp)), device_id_type=MESH)
    pl.semaphore_wait(barrier, n_vocab - 1 + n_dp - 1)

    sends = []

    def z_copy(src, h, b, side):
        peer = o + 1 if side == 0 else o - 1
        part = pl.ds(h * th, th)
        src = src.at[part] if src is hid else src.at[b, part]
        return rcopy(src, Hg.at[b, part], z_send.at[side, h, b], z_recv.at[h, b], (peer * 2 + i, r))

    for h in range(2):
        @pl.when(o < n_o - 1)
        def _():
            z_copy(hid, h, o, 0).start()

        @pl.when(o > 0)
        def _():
            z_copy(hid, h, o, 1).start()

    def z_step(h, d):
        @pl.when(o - d >= 0)
        def _():
            b = o - d
            z_copy(Hg, h, b, 0).wait_recv()

            @pl.when(o < n_o - 1)
            def _():
                z_copy(Hg, h, b, 0).start()

        @pl.when(o + d < n_o)
        def _():
            b = o + d
            z_copy(Hg, h, b, 1).wait_recv()

            @pl.when(o > 0)
            def _():
                z_copy(Hg, h, b, 1).start()

    def slot(ii, rr):
        return pl.ds(pl.multiple_of((ii * n_dp + rr) * rows, rows), rows)

    def w_slot(ii, rr):
        return Wg.at[:, slot(ii, rr), :]

    def w_sem(ii, rr):
        return w_recv.at[ii * n_dp + rr]

    def w_y(dy, k, ii):
        return rcopy(w_slot(ii, r), w_slot(ii, r), wy_send.at[dy - 1, k], w_sem(ii, r), y_peer(dy))

    def w_s(dy, k, ii):
        rr = y_at(dy) * 2 + c
        return rcopy(w_slot(ii, rr), w_slot(ii, rr), ws_send.at[dy, k], w_sem(ii, rr), sibling)

    def w_wait(ii, rr):
        rcopy(w_slot(ii, rr), w_slot(ii, rr), wx_send.at[0], w_sem(ii, rr), x_peer).wait_recv()

    for b in range(n_o):
        cols = pl.ds(pl.multiple_of((2 * b + 1 - i) * blk, blk), blk)
        wsend[b] = master[:, cols].astype(BF16)
    wx = rcopy(wsend, w_slot(i, r), wx_send.at[0], w_sem(i, r), x_peer)
    wx.start()
    sends.append(wx)
    for b in range(n_o):
        cols = pl.ds(pl.multiple_of((2 * b + i) * blk, blk), blk)
        Wg[b, slot(i, r), :] = master[:, cols].astype(BF16)
    for dy in range(1, n_y):
        q = w_y(dy, 0, i)
        q.start()
        sends.append(q)
    q = w_s(0, 0, i)
    q.start()
    sends.append(q)

    maskf = mask[...].astype(F32)
    cnt[r] = jnp.broadcast_to(jnp.sum(maskf, axis=1, keepdims=True), cnt.shape[1:])
    for k in range(1, n_dp):
        q = rcopy(cnt.at[r], cnt.at[r], c_send.at[k], c_recv.at[r], (v, lax.rem(r + k, n_dp)))
        q.start()
        sends.append(q)
    Hg[o] = hid[...]

    steps = [(h, d) for h in range(2) for d in range(1, n_o)]
    done = [0]

    def z_until(n):
        while done[0] < min(n, len(steps)):
            z_step(*steps[done[0]])
            done[0] += 1

    z_until(2)
    w_wait(1 - i, r)
    for dy in range(1, n_y):
        q = w_y(dy, 1, 1 - i)
        q.start()
        sends.append(q)
    q = w_s(0, 1, 1 - i)
    q.start()
    sends.append(q)
    for dy in range(1, n_y):
        w_wait(i, y_at(dy) * 2 + c)
        q = w_s(dy, 0, i)
        q.start()
        sends.append(q)
    z_until(n_o)
    for dy in range(1, n_y):
        w_wait(1 - i, y_at(dy) * 2 + c)
        q = w_s(dy, 1, 1 - i)
        q.start()
        sends.append(q)
    z_until(n_o + 1)
    for dy in range(n_y):
        for ii in range(2):
            w_wait(ii, y_at(dy) * 2 + 1 - c)

    def logits_of(h):
        part = slice(h * th, (h + 1) * th)
        total = None
        for b in range(n_o):
            term = lax.dot_general(
                Wg[b], Hg[b, part, :], (((1,), (1,)), ((), ())), preferred_element_type=F32
            )
            total = term if total is None else total + term
        acc[h] = total
        q = rcopy(acc.at[h], lrecv.at[h], l_send.at[h], l_recv.at[h], x_peer)
        q.start()
        return q

    def softmax_start(h, q):
        q.wait()
        part = slice(h * th, (h + 1) * th)
        logits = acc[h] + lrecv[h]
        acc[h] = logits
        ids = targets[:, part] - o * group
        hot = lax.broadcasted_iota(jnp.int32, (group, th), 0) == ids
        top = jnp.max(logits, axis=0, keepdims=True)
        stat[h, o] = jnp.zeros(stat.shape[2:], F32)
        stat[h, o, 0:1, :] = top
        stat[h, o, 1:2, :] = jnp.sum(jnp.exp(logits - top), axis=0, keepdims=True)
        stat[h, o, 2:3, :] = jnp.sum(jnp.where(hot, logits, 0.0), axis=0, keepdims=True)
        for k in range(1, n_o):
            dev = (lax.rem(o + k, n_o) * 2 + i, r)
            q = rcopy(stat.at[h, o], stat.at[h, o], st_send.at[h, k], st_recv.at[h, o], dev)
            q.start()
            sends.append(q)

    def softmax_end(h):
        part = slice(h * th, (h + 1) * th)
        for k in range(1, n_o):
            b = lax.rem(o + k, n_o)
            rcopy(stat.at[h, b], stat.at[h, b], st_send.at[h, k], st_recv.at[h, b], x_peer).wait_recv()
        row_top = stat[h, 0, 0:1, :]
        for b in range(1, n_o):
            row_top = jnp.maximum(row_top, stat[h, b, 0:1, :])
        exp_sum = jnp.zeros_like(row_top)
        picked = jnp.zeros_like(row_top)
        for b in range(n_o):
            exp_sum += stat[h, b, 1:2, :] * jnp.exp(stat[h, b, 0:1, :] - row_top)
            picked += stat[h, b, 2:3, :]
        log_norm = row_top + jnp.log(exp_sum)
        ids = targets[:, part] - o * group
        hot = (lax.broadcasted_iota(jnp.int32, (group, th), 0) == ids).astype(F32)
        grad = maskf[:, part] * (jnp.exp(acc[h] - log_norm) - hot)
        gt[:, part] = grad.astype(BF16)
        g_tv[part, :] = grad.T.astype(BF16)
        return jnp.sum(maskf[:, part] * (log_norm - picked), axis=1, keepdims=True)

    def hidden_terms(h):
        part = slice(h * th, (h + 1) * th)
        for k in sorted(range(1, n_o), key=lambda k: abs(2 * k - n_o)):
            b = lax.rem(o + k, n_o)
            htsend[h, k - 1] = jnp.dot(g_tv[part, :], Wg[b], preferred_element_type=F32).astype(BF16)
            q = ht_copy(h, k, (b * 2 + i, r))
            q.start()
            sends.append(q)

    def ht_copy(h, k, dev):
        return rcopy(
            htsend.at[h, k - 1], htrecv.at[h, k - 1], ht_send.at[h, k - 1], ht_recv.at[h, k - 1], dev
        )

    q0 = logits_of(0)
    z_until(len(steps))
    q1 = logits_of(1)
    softmax_start(0, q0)
    loss_local = softmax_end(0)
    hidden_terms(0)
    softmax_start(1, q1)
    loss_local = loss_local + softmax_end(1)

    m = 0
    for cc in (1 - c, c):
        for dy in list(range(1, n_y)) + [0]:
            for ii in (1 - i, i):
                gtp[m * rows:(m + 1) * rows, :] = gt[slot(ii, y_at(dy) * 2 + cc), :]
                m += 1
    mid = group // 2
    for b in range(n_o):
        gsend[b] = jnp.dot(gtp[:mid, :], Hg[b], preferred_element_type=F32).astype(BF16)
        q = rcopy(gsend.at[b], grecv.at[b], g_send.at[b], g_recv.at[b], sibling)
        q.start()
        sends.append(q)
    hidden_terms(1)
    for b in range(n_o):
        gown[b] = jnp.dot(gtp[mid:, :], Hg[b], preferred_element_type=F32)
    for b in range(n_o):
        rcopy(gsend.at[b], grecv.at[b], g_send.at[b], g_recv.at[b], sibling).wait_recv()
        for dy in range(1, n_y):
            part = slice((dy - 1) * 2 * rows, dy * 2 * rows)
            ysend[dy - 1, b] = (gown[b, part, :] + grecv[b, part, :].astype(F32)).astype(BF16)
            q = rcopy(
                ysend.at[dy - 1, b], yrecv.at[dy - 1, b], y_send.at[dy - 1, b], y_recv.at[dy - 1, b], y_peer(dy)
            )
            q.start()
            sends.append(q)
    last = slice((n_y - 1) * 2 * rows, n_y * 2 * rows)
    squares = jnp.zeros((8, blk), F32)
    for b in range(n_o):
        total = gown[b, last, :] + grecv[b, last, :].astype(F32)
        for dy in range(1, n_y):
            rcopy(
                ysend.at[dy - 1, b], yrecv.at[dy - 1, b], y_send.at[dy - 1, b], y_recv.at[dy - 1, b], y_peer(dy)
            ).wait_recv()
            total += yrecv[dy - 1, b].astype(F32)
        xsend[b] = total[:rows].astype(BF16)
        q = rcopy(xsend.at[b], xrecv.at[b], x_send.at[b], x_recv.at[b], x_peer)
        q.start()
        sends.append(q)
        mine = total[rows:]
        wgrad_out[:, pl.ds(pl.multiple_of((2 * b + i) * blk, blk), blk)] = mine
        squares += jnp.sum((mine * mine).reshape(rows // 8, 8, blk), axis=0)
    for b in range(n_o):
        rcopy(xsend.at[b], xrecv.at[b], x_send.at[b], x_recv.at[b], x_peer).wait_recv()
        theirs = xrecv[b].astype(F32)
        wgrad_out[:, pl.ds(pl.multiple_of((2 * b + 1 - i) * blk, blk), blk)] = theirs
        squares += jnp.sum((theirs * theirs).reshape(rows // 8, 8, blk), axis=0)
    square = jnp.sum(jnp.sum(squares, axis=0, keepdims=True), axis=1, keepdims=True)

    sqa[r, 0:8, :] = jnp.broadcast_to(square, (8, 128))
    sqa[r, 8:16, :] = jnp.broadcast_to(loss_local, (8, 128))
    for k in range(1, n_dp):
        q = rcopy(sqa.at[r], sqa.at[r], a_send.at[k], a_recv.at[r], (v, lax.rem(r + k, n_dp)))
        q.start()
        sends.append(q)
    for k in range(1, n_dp):
        b = lax.rem(r + k, n_dp)
        rcopy(sqa.at[b], sqa.at[b], a_send.at[k], a_recv.at[b], x_peer).wait_recv()
        rcopy(cnt.at[b], cnt.at[b], c_send.at[k], c_recv.at[b], x_peer).wait_recv()
    both = sqa[0]
    count = cnt[0]
    for b in range(1, n_dp):
        both = both + sqa[b]
        count = count + cnt[b]
    sqb[v] = both[0:8]
    for k in range(1, n_vocab):
        q = rcopy(sqb.at[v], sqb.at[v], b_send.at[k], b_recv.at[v], (lax.rem(v + k, n_vocab), r))
        q.start()
        sends.append(q)

    for h in range(2):
        part = slice(h * th, (h + 1) * th)
        total = jnp.dot(g_tv[part, :], Wg[o], preferred_element_type=F32)
        for k in range(1, n_o):
            ht_copy(h, k, x_peer).wait_recv()
            total += htrecv[h, k - 1].astype(F32)
        hgrad_out[part, :] = (total / count[0:1, 0:1]).astype(BF16)

    for k in range(1, n_vocab):
        b = lax.rem(v + k, n_vocab)
        rcopy(sqb.at[b], sqb.at[b], b_send.at[k], b_recv.at[b], x_peer).wait_recv()
    square_sum = sqb[0]
    for b in range(1, n_vocab):
        square_sum = square_sum + sqb[b]
    scal_out[0:8, :] = square_sum
    scal_out[8:16, :] = both[8:16]
    scal_out[16:24, :] = count

    for q in sends:
        q.wait_send()

    for h in range(2):
        @pl.when(o < n_o - 1)
        def _():
            z_copy(hid, h, o, 0).wait_send()

        @pl.when(o > 0)
        def _():
            z_copy(hid, h, o, 1).wait_send()

    for h, d in steps:
        @pl.when((o - d >= 0) & (o < n_o - 1))
        def _():
            z_copy(Hg, h, o - d, 0).wait_send()

        @pl.when((o + d < n_o) & (o > 0))
        def _():
            z_copy(Hg, h, o + d, 1).wait_send()


def on_device(hidden, targets, loss_mask, master, first_moment, second_moment):
    n_vocab, n_dp = lax.axis_size("vocab"), lax.axis_size("dp")
    n_o, n_y = n_vocab // 2, n_dp // 2
    toks, blk = hidden.shape
    rows, feats = master.shape
    group = 2 * n_dp * rows
    mid = group // 2
    vmem = pl.BlockSpec(memory_space=pltpu.VMEM)
    dma = pltpu.SemaphoreType.DMA
    arrays = [
        ((n_o, group, blk), BF16),
        ((n_o, rows, blk), BF16),
        ((n_o, toks, blk), BF16),
        ((2, group, toks // 2), F32),
        ((2, group, toks // 2), F32),
        ((group, toks), BF16),
        ((group, toks), BF16),
        ((toks, group), BF16),
        ((2, n_o - 1, toks // 2, blk), BF16),
        ((2, n_o - 1, toks // 2, blk), BF16),
        ((n_o, mid, blk), BF16),
        ((n_o, mid, blk), BF16),
        ((n_o, mid, blk), F32),
        ((n_y - 1, n_o, 2 * rows, blk), BF16),
        ((n_y - 1, n_o, 2 * rows, blk), BF16),
        ((n_o, rows, blk), BF16),
        ((n_o, rows, blk), BF16),
        ((2, n_o, 8, toks // 2), F32),
        ((n_dp, 8, 128), F32),
        ((n_dp, 16, 128), F32),
        ((n_vocab, 8, 128), F32),
    ]
    need = sum(math.prod(shape) * jnp.dtype(dtype).itemsize for shape, dtype in arrays)
    need += 2 * (rows * feats * 4 + toks * blk * 2) + (8 << 20)
    hidden_grad, weight_raw, scal = pl.pallas_call(
        functools.partial(kernel, n_vocab, n_dp),
        out_shape=(
            jax.ShapeDtypeStruct((toks, blk), BF16),
            jax.ShapeDtypeStruct((rows, feats), F32),
            jax.ShapeDtypeStruct((24, 128), F32),
        ),
        in_specs=[vmem] * 4,
        out_specs=(vmem, vmem, vmem),
        scratch_shapes=[pltpu.VMEM(shape, dtype) for shape, dtype in arrays] + [
            dma((2, 2, n_o)), dma((2, n_o)),
            dma((1,)), dma((n_y - 1, 2)), dma((n_y, 2)), dma((2 * n_dp,)),
            dma((2,)), dma((2,)),
            dma((2, n_o)), dma((2, n_o)),
            dma((2, n_o - 1)), dma((2, n_o - 1)),
            dma((n_o,)), dma((n_o,)),
            dma((n_y - 1, n_o)), dma((n_y - 1, n_o)),
            dma((n_o,)), dma((n_o,)),
            dma((n_dp,)), dma((n_dp,)),
            dma((n_dp,)), dma((n_dp,)),
            dma((n_vocab,)), dma((n_vocab,)),
        ],
        compiler_params=pltpu.CompilerParams(
            collective_id=0, has_side_effects=True, vmem_limit_bytes=need
        ),
        name="head",
    )(hidden, master, targets.reshape(1, toks), loss_mask.reshape(1, toks))
    square_sum, loss_sum, valid_count = scal[0, 0], scal[8, 0], scal[16, 0]
    loss_value = loss_sum / valid_count
    grad_norm = jnp.sqrt(square_sum) / valid_count
    clip_factor = jnp.minimum(1.0, clip_norm / (grad_norm + 1e-06))
    clipped = weight_raw / valid_count * clip_factor
    new_first = beta_one * first_moment + (1.0 - beta_one) * clipped
    new_second = beta_two * second_moment + (1.0 - beta_two) * clipped * clipped
    first_bias = 1.0 - beta_one**STEP
    second_bias = 1.0 - beta_two**STEP
    update = (
        new_first / first_bias / (jnp.sqrt(new_second / second_bias) + epsilon_adam)
        + decay_rate * master
    )
    new_master = master - learn_rate * update
    return (loss_value, hidden_grad, new_master, new_first, new_second)


def solution(mesh):
    placed = (
        P("dp", "vocab"),
        P("dp"),
        P("dp"),
        P(("vocab", "dp"), None),
        P(("vocab", "dp"), None),
        P(("vocab", "dp"), None),
    )
    return jax.shard_map(
        on_device,
        mesh=mesh,
        in_specs=placed,
        out_specs=(
            P(),
            P("dp", "vocab"),
            P(("vocab", "dp"), None),
            P(("vocab", "dp"), None),
            P(("vocab", "dp"), None),
        ),
        check_vma=False,
    )
```

```python
import functools

import jax
import jax.numpy as jnp
from jax import lax
from jax.experimental import pallas as pl
from jax.experimental.pallas import tpu as pltpu
from jax.sharding import PartitionSpec as P

STEP = 10

beta_one = 0.9
beta_two = 0.95
learn_rate = 0.0003
decay_rate = 0.1
epsilon_adam = 1e-08
clip_norm = 1.0

MESH = pl.DeviceIdType.MESH
F32 = jnp.float32
BF16 = jnp.bfloat16


def kernel(
    n_vocab, n_dp,
    hid, master_hbm, targets, mask,
    hgrad_out, wgrad_out, scal_out,
    master, hown, Wg, wsend, Hg, acc, lrecv, gt, gtp, g_tv,
    htsend, htrecv, gsend, grecv, gown, ysend, yrecv, xsend, xrecv,
    stat, cnt, sqa, sqb,
    in_sem, z_send, z_recv, wx_send, wy_send, ws_send, w_recv,
    l_send, l_recv, st_send, st_recv, ht_send, ht_recv,
    g_send, g_recv, y_send, y_recv, x_send, x_recv,
    c_send, c_recv, a_send, a_recv, b_send, b_recv,
):
    n_o = n_vocab // 2
    n_y = n_dp // 2
    v = lax.axis_index("vocab")
    r = lax.axis_index("dp")
    o = v // 2
    i = v % 2
    y = r // 2
    c = r % 2
    rows = master.shape[0]
    blk = hid.shape[1]
    toks = hid.shape[0]
    group = 2 * n_dp * rows
    th = toks // 2
    x_peer = (o * 2 + 1 - i, r)
    sibling = (v, y * 2 + 1 - c)

    def y_at(dy):
        return lax.rem(y + dy, n_y)

    def y_peer(dy):
        return (v, y_at(dy) * 2 + c)

    def rcopy(src, dst, ssem, rsem, dev):
        return pltpu.make_async_remote_copy(
            src_ref=src, dst_ref=dst, send_sem=ssem, recv_sem=rsem,
            device_id=dev, device_id_type=MESH,
        )

    load_master = pltpu.make_async_copy(master_hbm, master, in_sem.at[0])
    load_master.start()
    load_hid = pltpu.make_async_copy(hid, Hg.at[o], in_sem.at[1])
    load_hid.start()
    barrier = pltpu.get_barrier_semaphore()
    for k in range(1, n_vocab):
        pl.semaphore_signal(barrier, inc=1, device_id=(lax.rem(v + k, n_vocab), r), device_id_type=MESH)
    for k in range(1, n_dp):
        pl.semaphore_signal(barrier, inc=1, device_id=(v, lax.rem(r + k, n_dp)), device_id_type=MESH)
    pl.semaphore_wait(barrier, n_vocab - 1 + n_dp - 1)

    sends = []

    def z_copy(src, h, b, side):
        peer = o + 1 if side == 0 else o - 1
        part = pl.ds(h * th, th)
        src = src.at[part] if src is hid else src.at[b, part]
        return rcopy(src, Hg.at[b, part], z_send.at[side, h, b], z_recv.at[h, b], (peer * 2 + i, r))

    def z_own(h):
        @pl.when(o < n_o - 1)
        def _():
            z_copy(hid, h, o, 0).start()

        @pl.when(o > 0)
        def _():
            z_copy(hid, h, o, 1).start()

    def z_sent(h):
        @pl.when(o < n_o - 1)
        def _():
            z_copy(hid, h, o, 0).wait_send()

        @pl.when(o > 0)
        def _():
            z_copy(hid, h, o, 1).wait_send()

        for d in range(1, n_o):
            @pl.when((o - d >= 0) & (o < n_o - 1))
            def _():
                z_copy(Hg, h, o - d, 0).wait_send()

            @pl.when((o + d < n_o) & (o > 0))
            def _():
                z_copy(Hg, h, o + d, 1).wait_send()

    z_own(0)

    def z_step(h, d):
        @pl.when(o - d >= 0)
        def _():
            b = o - d
            z_copy(Hg, h, b, 0).wait_recv()

            @pl.when(o < n_o - 1)
            def _():
                z_copy(Hg, h, b, 0).start()

        @pl.when(o + d < n_o)
        def _():
            b = o + d
            z_copy(Hg, h, b, 1).wait_recv()

            @pl.when(o > 0)
            def _():
                z_copy(Hg, h, b, 1).start()

    def slot(ii, rr):
        return pl.ds(pl.multiple_of((ii * n_dp + rr) * rows, rows), rows)

    def w_slot(ii, rr):
        return Wg.at[:, slot(ii, rr), :]

    def w_sem(ii, rr):
        return w_recv.at[ii * n_dp + rr]

    def w_y(dy, k, ii):
        return rcopy(w_slot(ii, r), w_slot(ii, r), wy_send.at[dy - 1, k], w_sem(ii, r), y_peer(dy))

    def w_s(dy, k, ii):
        rr = y_at(dy) * 2 + c
        return rcopy(w_slot(ii, rr), w_slot(ii, rr), ws_send.at[dy, k], w_sem(ii, rr), sibling)

    def w_wait(ii, rr):
        rcopy(w_slot(ii, rr), w_slot(ii, rr), wx_send.at[0], w_sem(ii, rr), x_peer).wait_recv()

    load_master.wait()
    for b in range(n_o):
        cols = pl.ds(pl.multiple_of((2 * b + 1 - i) * blk, blk), blk)
        wsend[b] = master[:, cols].astype(BF16)
    wx = rcopy(wsend, w_slot(i, r), wx_send.at[0], w_sem(i, r), x_peer)
    wx.start()
    sends.append(wx)
    for b in range(n_o):
        cols = pl.ds(pl.multiple_of((2 * b + i) * blk, blk), blk)
        Wg[b, slot(i, r), :] = master[:, cols].astype(BF16)
    for dy in range(1, n_y):
        q = w_y(dy, 0, i)
        q.start()
        sends.append(q)
    q = w_s(0, 0, i)
    q.start()
    sends.append(q)

    maskf = mask[...].astype(F32)
    cnt[r] = jnp.broadcast_to(jnp.sum(maskf, axis=1, keepdims=True), cnt.shape[1:])
    for k in range(1, n_dp):
        q = rcopy(cnt.at[r], cnt.at[r], c_send.at[k], c_recv.at[r], (v, lax.rem(r + k, n_dp)))
        q.start()
        sends.append(q)
    load_hid.wait()

    steps = [(h, d) for h in range(2) for d in range(1, n_o)]
    done = [0]

    def z_until(n):
        while done[0] < min(n, len(steps)):
            z_step(*steps[done[0]])
            done[0] += 1

    z_until(2)
    w_wait(1 - i, r)
    for dy in range(1, n_y):
        q = w_y(dy, 1, 1 - i)
        q.start()
        sends.append(q)
    q = w_s(0, 1, 1 - i)
    q.start()
    sends.append(q)
    for dy in range(1, n_y):
        w_wait(i, y_at(dy) * 2 + c)
        q = w_s(dy, 0, i)
        q.start()
        sends.append(q)
    z_until(n_o - 1)
    z_sent(0)
    z_own(1)
    z_until(n_o)
    for dy in range(1, n_y):
        w_wait(1 - i, y_at(dy) * 2 + c)
        q = w_s(dy, 1, 1 - i)
        q.start()
        sends.append(q)
    for dy in range(n_y):
        for ii in range(2):
            w_wait(ii, y_at(dy) * 2 + 1 - c)

    def logits_of(h):
        part = slice(h * th, (h + 1) * th)
        total = None
        for b in range(n_o):
            term = lax.dot_general(
                Wg[b], Hg[b, part, :], (((1,), (1,)), ((), ())), preferred_element_type=F32
            )
            total = term if total is None else total + term
        acc[h] = total
        q = rcopy(acc.at[h], lrecv.at[h], l_send.at[h], l_recv.at[h], x_peer)
        q.start()
        return q

    def softmax_start(h, q):
        q.wait()
        part = slice(h * th, (h + 1) * th)
        logits = acc[h] + lrecv[h]
        acc[h] = logits
        ids = targets[:, part] - o * group
        hot = lax.broadcasted_iota(jnp.int32, (group, th), 0) == ids
        top = jnp.max(logits, axis=0, keepdims=True)
        stat[h, o] = jnp.zeros(stat.shape[2:], F32)
        stat[h, o, 0:1, :] = top
        stat[h, o, 1:2, :] = jnp.sum(jnp.exp(logits - top), axis=0, keepdims=True)
        stat[h, o, 2:3, :] = jnp.sum(jnp.where(hot, logits, 0.0), axis=0, keepdims=True)
        for k in range(1, n_o):
            dev = (lax.rem(o + k, n_o) * 2 + i, r)
            q = rcopy(stat.at[h, o], stat.at[h, o], st_send.at[h, k], st_recv.at[h, o], dev)
            q.start()
            sends.append(q)

    def softmax_end(h):
        part = slice(h * th, (h + 1) * th)
        for k in range(1, n_o):
            b = lax.rem(o + k, n_o)
            rcopy(stat.at[h, b], stat.at[h, b], st_send.at[h, k], st_recv.at[h, b], x_peer).wait_recv()
        row_top = stat[h, 0, 0:1, :]
        for b in range(1, n_o):
            row_top = jnp.maximum(row_top, stat[h, b, 0:1, :])
        exp_sum = jnp.zeros_like(row_top)
        picked = jnp.zeros_like(row_top)
        for b in range(n_o):
            exp_sum += stat[h, b, 1:2, :] * jnp.exp(stat[h, b, 0:1, :] - row_top)
            picked += stat[h, b, 2:3, :]
        log_norm = row_top + jnp.log(exp_sum)
        ids = targets[:, part] - o * group
        hot = (lax.broadcasted_iota(jnp.int32, (group, th), 0) == ids).astype(F32)
        grad = maskf[:, part] * (jnp.exp(acc[h] - log_norm) - hot)
        gt[:, part] = grad.astype(BF16)
        g_tv[part, :] = grad.T.astype(BF16)
        return jnp.sum(maskf[:, part] * (log_norm - picked), axis=1, keepdims=True)

    def hidden_terms(h):
        part = slice(h * th, (h + 1) * th)
        for k in sorted(range(1, n_o), key=lambda k: abs(2 * k - n_o)):
            b = lax.rem(o + k, n_o)
            htsend[h, k - 1] = jnp.dot(g_tv[part, :], Wg[b], preferred_element_type=F32).astype(BF16)
            q = ht_copy(h, k, (b * 2 + i, r))
            q.start()
            sends.append(q)

    def ht_copy(h, k, dev):
        return rcopy(
            htsend.at[h, k - 1], htrecv.at[h, k - 1], ht_send.at[h, k - 1], ht_recv.at[h, k - 1], dev
        )

    q0 = logits_of(0)
    z_until(len(steps) - 1)
    softmax_start(0, q0)
    z_until(len(steps))
    q1 = logits_of(1)
    loss_local = softmax_end(0)
    hidden_terms(0)
    softmax_start(1, q1)
    loss_local = loss_local + softmax_end(1)

    m = 0
    for cc in (1 - c, c):
        for dy in list(range(1, n_y)) + [0]:
            for ii in (1 - i, i):
                gtp[m * rows:(m + 1) * rows, :] = gt[slot(ii, y_at(dy) * 2 + cc), :]
                m += 1
    mid = group // 2
    for b in range(n_o):
        gsend[b] = jnp.dot(gtp[:mid, :], Hg[b], preferred_element_type=F32).astype(BF16)
        q = rcopy(gsend.at[b], grecv.at[b], g_send.at[b], g_recv.at[b], sibling)
        q.start()
        sends.append(q)
    hidden_terms(1)
    for b in range(n_o):
        gown[b] = jnp.dot(gtp[mid:, :], Hg[b], preferred_element_type=F32)
    for h in range(2):
        hown[h] = jnp.dot(g_tv[h * th:(h + 1) * th, :], Wg[o], preferred_element_type=F32)

    def y_copy(dy, ii, b):
        return rcopy(
            ysend.at[dy - 1, ii, b], yrecv.at[dy - 1, ii, b],
            y_send.at[dy - 1, ii, b], y_recv.at[dy - 1, ii, b], y_peer(dy),
        )

    def two_cores(dy, ii, b):
        at = ((dy - 1) * 2 + ii) * rows
        return gown[b, at:at + rows, :] + grecv[b, at:at + rows, :].astype(F32)

    def y_start(dy, ii, b):
        ysend[dy - 1, ii, b] = two_cores(dy, ii, b).astype(BF16)
        q = y_copy(dy, ii, b)
        q.start()
        sends.append(q)

    for b in range(n_o):
        rcopy(gsend.at[b], grecv.at[b], g_send.at[b], g_recv.at[b], sibling).wait_recv()
        for dy in range(1, n_y):
            y_start(dy, 0, b)
    squares = jnp.zeros((8, blk), F32)
    for b in range(n_o):
        total = two_cores(n_y, 0, b)
        for dy in range(1, n_y):
            y_copy(dy, 0, b).wait_recv()
            y_start(dy, 1, b)
            total += yrecv[dy - 1, 0, b].astype(F32)
        xsend[b] = total.astype(BF16)
        q = rcopy(xsend.at[b], xrecv.at[b], x_send.at[b], x_recv.at[b], x_peer)
        q.start()
        sends.append(q)
    for b in range(n_o):
        mine = two_cores(n_y, 1, b)
        for dy in range(1, n_y):
            y_copy(dy, 1, b).wait_recv()
            mine += yrecv[dy - 1, 1, b].astype(F32)
        wgrad_out[:, pl.ds(pl.multiple_of((2 * b + i) * blk, blk), blk)] = mine
        squares += jnp.sum((mine * mine).reshape(rows // 8, 8, blk), axis=0)
    for b in range(n_o):
        rcopy(xsend.at[b], xrecv.at[b], x_send.at[b], x_recv.at[b], x_peer).wait_recv()
        theirs = xrecv[b].astype(F32)
        wgrad_out[:, pl.ds(pl.multiple_of((2 * b + 1 - i) * blk, blk), blk)] = theirs
        squares += jnp.sum((theirs * theirs).reshape(rows // 8, 8, blk), axis=0)
    square = jnp.sum(jnp.sum(squares, axis=0, keepdims=True), axis=1, keepdims=True)

    sqa[r, 0:8, :] = jnp.broadcast_to(square, (8, 128))
    sqa[r, 8:16, :] = jnp.broadcast_to(loss_local, (8, 128))
    for k in range(1, n_dp):
        q = rcopy(sqa.at[r], sqa.at[r], a_send.at[k], a_recv.at[r], (v, lax.rem(r + k, n_dp)))
        q.start()
        sends.append(q)
    for k in range(1, n_dp):
        b = lax.rem(r + k, n_dp)
        rcopy(sqa.at[b], sqa.at[b], a_send.at[k], a_recv.at[b], x_peer).wait_recv()
        rcopy(cnt.at[b], cnt.at[b], c_send.at[k], c_recv.at[b], x_peer).wait_recv()
    both = sqa[0]
    count = cnt[0]
    for b in range(1, n_dp):
        both = both + sqa[b]
        count = count + cnt[b]
    sqb[v] = both[0:8]
    for k in range(1, n_vocab):
        q = rcopy(sqb.at[v], sqb.at[v], b_send.at[k], b_recv.at[v], (lax.rem(v + k, n_vocab), r))
        q.start()
        sends.append(q)

    for h in range(2):
        part = slice(h * th, (h + 1) * th)
        total = hown[h]
        for k in range(1, n_o):
            ht_copy(h, k, x_peer).wait_recv()
            total += htrecv[h, k - 1].astype(F32)
        hgrad_out[part, :] = (total / count[0:1, 0:1]).astype(BF16)

    for k in range(1, n_vocab):
        b = lax.rem(v + k, n_vocab)
        rcopy(sqb.at[b], sqb.at[b], b_send.at[k], b_recv.at[b], x_peer).wait_recv()
    square_sum = sqb[0]
    for b in range(1, n_vocab):
        square_sum = square_sum + sqb[b]
    norm = jnp.sqrt(square_sum) / count
    factor = jnp.minimum(1.0, clip_norm / (norm + 1e-06)) / count
    scal_out[...] = both[8:16] / count
    for b in range(n_vocab):
        part = slice(b * blk, (b + 1) * blk)
        wgrad_out[:, part] = wgrad_out[:, part] * factor[0:1, 0:1]

    for q in sends:
        q.wait_send()
    z_sent(1)


def on_device(hidden, targets, loss_mask, master, first_moment, second_moment):
    n_vocab, n_dp = lax.axis_size("vocab"), lax.axis_size("dp")
    n_o, n_y = n_vocab // 2, n_dp // 2
    toks, blk = hidden.shape
    rows, feats = master.shape
    group = 2 * n_dp * rows
    mid = group // 2
    vmem = pl.BlockSpec(memory_space=pltpu.VMEM)
    dma = pltpu.SemaphoreType.DMA
    arrays = [
        ((rows, feats), F32),
        ((2, toks // 2, blk), F32),
        ((n_o, group, blk), BF16),
        ((n_o, rows, blk), BF16),
        ((n_o, toks, blk), BF16),
        ((2, group, toks // 2), F32),
        ((2, group, toks // 2), F32),
        ((group, toks), BF16),
        ((group, toks), BF16),
        ((toks, group), BF16),
        ((2, n_o - 1, toks // 2, blk), BF16),
        ((2, n_o - 1, toks // 2, blk), BF16),
        ((n_o, mid, blk), BF16),
        ((n_o, mid, blk), BF16),
        ((n_o, mid, blk), F32),
        ((n_y - 1, 2, n_o, rows, blk), BF16),
        ((n_y - 1, 2, n_o, rows, blk), BF16),
        ((n_o, rows, blk), BF16),
        ((n_o, rows, blk), BF16),
        ((2, n_o, 8, toks // 2), F32),
        ((n_dp, 8, 128), F32),
        ((n_dp, 16, 128), F32),
        ((n_vocab, 8, 128), F32),
    ]
    hidden_grad, clipped, scal = pl.pallas_call(
        functools.partial(kernel, n_vocab, n_dp),
        out_shape=(
            jax.ShapeDtypeStruct((toks, blk), BF16),
            jax.ShapeDtypeStruct((rows, feats), F32),
            jax.ShapeDtypeStruct((8, 128), F32),
        ),
        in_specs=[pl.BlockSpec(memory_space=pl.ANY)] * 2 + [vmem] * 2,
        out_specs=(vmem, vmem, vmem),
        scratch_shapes=[pltpu.VMEM(shape, dtype) for shape, dtype in arrays] + [
            dma((2,)), dma((2, 2, n_o)), dma((2, n_o)),
            dma((1,)), dma((n_y - 1, 2)), dma((n_y, 2)), dma((2 * n_dp,)),
            dma((2,)), dma((2,)),
            dma((2, n_o)), dma((2, n_o)),
            dma((2, n_o - 1)), dma((2, n_o - 1)),
            dma((n_o,)), dma((n_o,)),
            dma((n_y - 1, 2, n_o)), dma((n_y - 1, 2, n_o)),
            dma((n_o,)), dma((n_o,)),
            dma((n_dp,)), dma((n_dp,)),
            dma((n_dp,)), dma((n_dp,)),
            dma((n_vocab,)), dma((n_vocab,)),
        ],
        compiler_params=pltpu.CompilerParams(
            collective_id=0, has_side_effects=True, vmem_limit_bytes=60 * 1024 * 1024
        ),
        name="head",
    )(hidden, master, targets.reshape(1, toks), loss_mask.reshape(1, toks))
    loss_value = scal[0, 0]
    new_first = beta_one * first_moment + (1.0 - beta_one) * clipped
    new_second = beta_two * second_moment + (1.0 - beta_two) * clipped * clipped
    first_scale = learn_rate / (1.0 - beta_one**STEP)
    second_scale = 1.0 / (1.0 - beta_two**STEP)
    new_master = master * (1.0 - learn_rate * decay_rate) - first_scale * new_first / (
        jnp.sqrt(second_scale * new_second) + epsilon_adam
    )
    return (loss_value, hidden_grad, new_master, new_first, new_second)


def solution(mesh):
    placed = (
        P("dp", "vocab"),
        P("dp"),
        P("dp"),
        P(("vocab", "dp"), None),
        P(("vocab", "dp"), None),
        P(("vocab", "dp"), None),
    )
    return jax.shard_map(
        on_device,
        mesh=mesh,
        in_specs=placed,
        out_specs=(
            P(),
            P("dp", "vocab"),
            P(("vocab", "dp"), None),
            P(("vocab", "dp"), None),
            P(("vocab", "dp"), None),
        ),
        check_vma=False,
    )
```

```python
import functools

import jax
import jax.numpy as jnp
from jax import lax
from jax.experimental import pallas as pl
from jax.experimental.pallas import tpu as pltpu
from jax.sharding import PartitionSpec as P

STEP = 10

beta_one = 0.9
beta_two = 0.95
learn_rate = 0.0003
decay_rate = 0.1
epsilon_adam = 1e-08
clip_norm = 1.0

MESH = pl.DeviceIdType.MESH
F32 = jnp.float32
BF16 = jnp.bfloat16


def kernel(
    n_vocab, n_dp,
    hid, master_hbm, targets, mask,
    hgrad_out, wgrad_out, scal_out,
    master, hterm, Wg, wsend, Hg, acc, lrecv, gt, gtp, g_tv,
    hsend, hrecv, gsend, grecv, gown, ysend, yrecv, xsend, xrecv,
    stat, cnt, sqa, sqb,
    in_sem, z_send, z_recv, wx_send, wy_send, ws_send, w_recv,
    l_send, l_recv, st_send, st_recv, ht_send, ht_recv,
    g_send, g_recv, y_send, y_recv, x_send, x_recv,
    c_send, c_recv, a_send, a_recv, b_send, b_recv,
):
    n_o = n_vocab // 2
    n_y = n_dp // 2
    v = lax.axis_index("vocab")
    r = lax.axis_index("dp")
    o = v // 2
    i = v % 2
    y = r // 2
    c = r % 2
    rows = master.shape[0]
    blk = hid.shape[1]
    toks = hid.shape[0]
    group = 2 * n_dp * rows
    th = toks // 2
    x_peer = (o * 2 + 1 - i, r)
    sibling = (v, y * 2 + 1 - c)

    def y_at(dy):
        return lax.rem(y + dy, n_y)

    def y_peer(dy):
        return (v, y_at(dy) * 2 + c)

    def rcopy(src, dst, ssem, rsem, dev):
        return pltpu.make_async_remote_copy(
            src_ref=src, dst_ref=dst, send_sem=ssem, recv_sem=rsem,
            device_id=dev, device_id_type=MESH,
        )

    load_master = pltpu.make_async_copy(master_hbm, master, in_sem.at[0])
    load_master.start()
    load_hid = pltpu.make_async_copy(hid, Hg.at[o], in_sem.at[1])
    load_hid.start()
    barrier = pltpu.get_barrier_semaphore()
    for k in range(1, n_vocab):
        pl.semaphore_signal(barrier, inc=1, device_id=(lax.rem(v + k, n_vocab), r), device_id_type=MESH)
    for k in range(1, n_dp):
        pl.semaphore_signal(barrier, inc=1, device_id=(v, lax.rem(r + k, n_dp)), device_id_type=MESH)
    pl.semaphore_wait(barrier, n_vocab - 1 + n_dp - 1)

    sends = []

    def z_copy(src, h, b, side):
        peer = o + 1 if side == 0 else o - 1
        part = pl.ds(h * th, th)
        src = src.at[part] if src is hid else src.at[b, part]
        return rcopy(src, Hg.at[b, part], z_send.at[side, h, b], z_recv.at[h, b], (peer * 2 + i, r))

    def z_own(h):
        @pl.when(o < n_o - 1)
        def _():
            z_copy(hid, h, o, 0).start()

        @pl.when(o > 0)
        def _():
            z_copy(hid, h, o, 1).start()

    def z_sent(h):
        @pl.when(o < n_o - 1)
        def _():
            z_copy(hid, h, o, 0).wait_send()

        @pl.when(o > 0)
        def _():
            z_copy(hid, h, o, 1).wait_send()

        for d in range(1, n_o):
            @pl.when((o - d >= 0) & (o < n_o - 1))
            def _():
                z_copy(Hg, h, o - d, 0).wait_send()

            @pl.when((o + d < n_o) & (o > 0))
            def _():
                z_copy(Hg, h, o + d, 1).wait_send()

    z_own(0)

    def z_step(h, d):
        @pl.when(o - d >= 0)
        def _():
            b = o - d
            z_copy(Hg, h, b, 0).wait_recv()

            @pl.when(o < n_o - 1)
            def _():
                z_copy(Hg, h, b, 0).start()

        @pl.when(o + d < n_o)
        def _():
            b = o + d
            z_copy(Hg, h, b, 1).wait_recv()

            @pl.when(o > 0)
            def _():
                z_copy(Hg, h, b, 1).start()

    def slot(ii, rr):
        return pl.ds(pl.multiple_of((ii * n_dp + rr) * rows, rows), rows)

    def w_slot(ii, rr):
        return Wg.at[:, slot(ii, rr), :]

    def w_sem(ii, rr):
        return w_recv.at[ii * n_dp + rr]

    def w_y(dy, k, ii):
        return rcopy(w_slot(ii, r), w_slot(ii, r), wy_send.at[dy - 1, k], w_sem(ii, r), y_peer(dy))

    def w_s(dy, k, ii):
        rr = y_at(dy) * 2 + c
        return rcopy(w_slot(ii, rr), w_slot(ii, rr), ws_send.at[dy, k], w_sem(ii, rr), sibling)

    def w_wait(ii, rr):
        rcopy(w_slot(ii, rr), w_slot(ii, rr), wx_send.at[0], w_sem(ii, rr), x_peer).wait_recv()

    load_master.wait()
    for b in range(n_o):
        cols = pl.ds(pl.multiple_of((2 * b + 1 - i) * blk, blk), blk)
        wsend[b] = master[:, cols].astype(BF16)
    wx = rcopy(wsend, w_slot(i, r), wx_send.at[0], w_sem(i, r), x_peer)
    wx.start()
    sends.append(wx)
    for b in range(n_o):
        cols = pl.ds(pl.multiple_of((2 * b + i) * blk, blk), blk)
        Wg[b, slot(i, r), :] = master[:, cols].astype(BF16)
    for dy in range(1, n_y):
        q = w_y(dy, 0, i)
        q.start()
        sends.append(q)
    q = w_s(0, 0, i)
    q.start()
    sends.append(q)

    maskf = mask[...].astype(F32)
    cnt[r] = jnp.broadcast_to(jnp.sum(maskf, axis=1, keepdims=True), cnt.shape[1:])
    for k in range(1, n_dp):
        q = rcopy(cnt.at[r], cnt.at[r], c_send.at[k], c_recv.at[r], (v, lax.rem(r + k, n_dp)))
        q.start()
        sends.append(q)
    load_hid.wait()

    steps = [(h, d) for h in range(2) for d in range(1, n_o)]
    done = [0]

    def z_until(n):
        while done[0] < min(n, len(steps)):
            z_step(*steps[done[0]])
            done[0] += 1

    z_until(2)
    w_wait(1 - i, r)
    for dy in range(1, n_y):
        q = w_y(dy, 1, 1 - i)
        q.start()
        sends.append(q)
    q = w_s(0, 1, 1 - i)
    q.start()
    sends.append(q)
    for dy in range(1, n_y):
        w_wait(i, y_at(dy) * 2 + c)
        q = w_s(dy, 0, i)
        q.start()
        sends.append(q)
    z_until(n_o - 1)
    z_sent(0)
    z_own(1)
    z_until(n_o)
    for dy in range(1, n_y):
        w_wait(1 - i, y_at(dy) * 2 + c)
        q = w_s(dy, 1, 1 - i)
        q.start()
        sends.append(q)
    for dy in range(n_y):
        for ii in range(2):
            w_wait(ii, y_at(dy) * 2 + 1 - c)

    def logits_of(h):
        part = slice(h * th, (h + 1) * th)
        total = None
        for b in range(n_o):
            term = lax.dot_general(
                Wg[b], Hg[b, part, :], (((1,), (1,)), ((), ())), preferred_element_type=F32
            )
            total = term if total is None else total + term
        acc[h] = total
        q = rcopy(acc.at[h], lrecv.at[h], l_send.at[h], l_recv.at[h], x_peer)
        q.start()
        return q

    def softmax_start(h, q):
        q.wait()
        part = slice(h * th, (h + 1) * th)
        logits = acc[h] + lrecv[h]
        acc[h] = logits
        ids = targets[:, part] - o * group
        hot = lax.broadcasted_iota(jnp.int32, (group, th), 0) == ids
        top = jnp.max(logits, axis=0, keepdims=True)
        stat[h, o] = jnp.zeros(stat.shape[2:], F32)
        stat[h, o, 0:1, :] = top
        stat[h, o, 1:2, :] = jnp.sum(jnp.exp(logits - top), axis=0, keepdims=True)
        stat[h, o, 2:3, :] = jnp.sum(jnp.where(hot, logits, 0.0), axis=0, keepdims=True)
        for k in range(1, n_o):
            dev = (lax.rem(o + k, n_o) * 2 + i, r)
            q = rcopy(stat.at[h, o], stat.at[h, o], st_send.at[h, k], st_recv.at[h, o], dev)
            q.start()
            sends.append(q)

    def softmax_end(h):
        part = slice(h * th, (h + 1) * th)
        for k in range(1, n_o):
            b = lax.rem(o + k, n_o)
            rcopy(stat.at[h, b], stat.at[h, b], st_send.at[h, k], st_recv.at[h, b], x_peer).wait_recv()
        row_top = stat[h, 0, 0:1, :]
        for b in range(1, n_o):
            row_top = jnp.maximum(row_top, stat[h, b, 0:1, :])
        exp_sum = jnp.zeros_like(row_top)
        picked = jnp.zeros_like(row_top)
        for b in range(n_o):
            exp_sum += stat[h, b, 1:2, :] * jnp.exp(stat[h, b, 0:1, :] - row_top)
            picked += stat[h, b, 2:3, :]
        log_norm = row_top + jnp.log(exp_sum)
        ids = targets[:, part] - o * group
        hot = (lax.broadcasted_iota(jnp.int32, (group, th), 0) == ids).astype(F32)
        grad = maskf[:, part] * (jnp.exp(acc[h] - log_norm) - hot)
        gt[:, part] = grad.astype(BF16)
        g_tv[part, :] = grad.T.astype(BF16)
        return jnp.sum(maskf[:, part] * (log_norm - picked), axis=1, keepdims=True)

    def hidden_terms(h):
        part = slice(h * th, (h + 1) * th)
        for k in range(n_o):
            b = lax.rem(o + k, n_o)
            hterm[h, b] = jnp.dot(g_tv[part, :], Wg[b], preferred_element_type=F32)

    def ht_copy(h, b, side):
        if side == 0:
            to, at = o + 1, b
        else:
            to, at = o - 1, jnp.where(b == o - 1, n_o, b)
        return rcopy(hsend.at[h, b], hrecv.at[h, at], ht_send.at[h, b], ht_recv.at[h, at], (to * 2 + i, r))

    def ht_wait(h, at):
        rcopy(hsend.at[h, 0], hrecv.at[h, at], ht_send.at[h, 0], ht_recv.at[h, at], x_peer).wait_recv()

    def ht_step(h, s):
        for side in range(2):
            place = o if side == 0 else n_o - 1 - o
            b = n_o - s + o if side == 0 else s - 1 - place

            @pl.when(place < s)
            def _():
                @pl.when(place + 1 < s)
                def _():
                    ht_copy(h, b + 1 if side == 0 else b - 1, side).wait_send()

                @pl.when(place > 0)
                def _():
                    ht_wait(h, b)
                    hsend[h, b] = (hterm[h, b] + hrecv[h, b].astype(F32)).astype(BF16)

                @pl.when(place == 0)
                def _():
                    hsend[h, b] = hterm[h, b].astype(BF16)

                ht_copy(h, b, side).start()

    def ht_finish(h):
        @pl.when(o > 0)
        def _():
            ht_wait(h, o)
            hterm[h, o] = hterm[h, o] + hrecv[h, o].astype(F32)

        @pl.when(o < n_o - 1)
        def _():
            ht_wait(h, n_o)
            hterm[h, o] = hterm[h, o] + hrecv[h, n_o].astype(F32)

    def ht_sent(h):
        for side in range(2):
            place = o if side == 0 else n_o - 1 - o

            @pl.when(place < n_o - 1)
            def _():
                ht_copy(h, o + 1 if side == 0 else o - 1, side).wait_send()

    ht_steps = [(h, s) for h in range(2) for s in range(1, n_o)]
    ht_done = [0]

    def ht_until(n):
        while ht_done[0] < min(n, len(ht_steps)):
            ht_step(*ht_steps[ht_done[0]])
            ht_done[0] += 1

    q0 = logits_of(0)
    z_until(len(steps) - 1)
    softmax_start(0, q0)
    z_until(len(steps))
    q1 = logits_of(1)
    loss_local = softmax_end(0)
    hidden_terms(0)
    ht_until(1)
    softmax_start(1, q1)
    ht_until(2)
    loss_local = loss_local + softmax_end(1)

    m = 0
    for cc in (1 - c, c):
        for dy in list(range(1, n_y)) + [0]:
            for ii in (1 - i, i):
                gtp[m * rows:(m + 1) * rows, :] = gt[slot(ii, y_at(dy) * 2 + cc), :]
                m += 1
    mid = group // 2
    for b in range(n_o):
        gsend[b] = jnp.dot(gtp[:mid, :], Hg[b], preferred_element_type=F32).astype(BF16)
        q = rcopy(gsend.at[b], grecv.at[b], g_send.at[b], g_recv.at[b], sibling)
        q.start()
        sends.append(q)
    ht_until(n_o - 1)
    hidden_terms(1)
    ht_until(n_o)
    for b in range(n_o):
        gown[b] = jnp.dot(gtp[mid:, :], Hg[b], preferred_element_type=F32)
    def y_copy(dy, ii, b):
        return rcopy(
            ysend.at[dy - 1, ii, b], yrecv.at[dy - 1, ii, b],
            y_send.at[dy - 1, ii, b], y_recv.at[dy - 1, ii, b], y_peer(dy),
        )

    def two_cores(dy, ii, b):
        at = ((dy - 1) * 2 + ii) * rows
        return gown[b, at:at + rows, :] + grecv[b, at:at + rows, :].astype(F32)

    def y_start(dy, ii, b):
        ysend[dy - 1, ii, b] = two_cores(dy, ii, b).astype(BF16)
        q = y_copy(dy, ii, b)
        q.start()
        sends.append(q)

    for b in range(n_o):
        rcopy(gsend.at[b], grecv.at[b], g_send.at[b], g_recv.at[b], sibling).wait_recv()
        for dy in range(1, n_y):
            y_start(dy, 0, b)
    ht_until(n_o + 1)
    squares = jnp.zeros((8, blk), F32)
    for b in range(n_o):
        total = two_cores(n_y, 0, b)
        for dy in range(1, n_y):
            y_copy(dy, 0, b).wait_recv()
            y_start(dy, 1, b)
            total += yrecv[dy - 1, 0, b].astype(F32)
        xsend[b] = total.astype(BF16)
        q = rcopy(xsend.at[b], xrecv.at[b], x_send.at[b], x_recv.at[b], x_peer)
        q.start()
        sends.append(q)
    ht_until(len(ht_steps))
    for b in range(n_o):
        mine = two_cores(n_y, 1, b)
        for dy in range(1, n_y):
            y_copy(dy, 1, b).wait_recv()
            mine += yrecv[dy - 1, 1, b].astype(F32)
        wgrad_out[:, pl.ds(pl.multiple_of((2 * b + i) * blk, blk), blk)] = mine
        squares += jnp.sum((mine * mine).reshape(rows // 8, 8, blk), axis=0)
    for b in range(n_o):
        rcopy(xsend.at[b], xrecv.at[b], x_send.at[b], x_recv.at[b], x_peer).wait_recv()
        theirs = xrecv[b].astype(F32)
        wgrad_out[:, pl.ds(pl.multiple_of((2 * b + 1 - i) * blk, blk), blk)] = theirs
        squares += jnp.sum((theirs * theirs).reshape(rows // 8, 8, blk), axis=0)
    square = jnp.sum(jnp.sum(squares, axis=0, keepdims=True), axis=1, keepdims=True)

    sqa[r, 0:8, :] = jnp.broadcast_to(square, (8, 128))
    sqa[r, 8:16, :] = jnp.broadcast_to(loss_local, (8, 128))
    for k in range(1, n_dp):
        q = rcopy(sqa.at[r], sqa.at[r], a_send.at[k], a_recv.at[r], (v, lax.rem(r + k, n_dp)))
        q.start()
        sends.append(q)
    for k in range(1, n_dp):
        b = lax.rem(r + k, n_dp)
        rcopy(sqa.at[b], sqa.at[b], a_send.at[k], a_recv.at[b], x_peer).wait_recv()
        rcopy(cnt.at[b], cnt.at[b], c_send.at[k], c_recv.at[b], x_peer).wait_recv()
    both = sqa[0]
    count = cnt[0]
    for b in range(1, n_dp):
        both = both + sqa[b]
        count = count + cnt[b]
    sqb[v] = both[0:8]
    for k in range(1, n_vocab):
        q = rcopy(sqb.at[v], sqb.at[v], b_send.at[k], b_recv.at[v], (lax.rem(v + k, n_vocab), r))
        q.start()
        sends.append(q)

    for h in range(2):
        part = slice(h * th, (h + 1) * th)
        ht_finish(h)
        hgrad_out[part, :] = (hterm[h, o] / count[0:1, 0:1]).astype(BF16)

    for k in range(1, n_vocab):
        b = lax.rem(v + k, n_vocab)
        rcopy(sqb.at[b], sqb.at[b], b_send.at[k], b_recv.at[b], x_peer).wait_recv()
    square_sum = sqb[0]
    for b in range(1, n_vocab):
        square_sum = square_sum + sqb[b]
    norm = jnp.sqrt(square_sum) / count
    factor = jnp.minimum(1.0, clip_norm / (norm + 1e-06)) / count
    scal_out[...] = (both[8:16] / count)[0:1, 0:1]
    for b in range(n_vocab):
        part = slice(b * blk, (b + 1) * blk)
        wgrad_out[:, part] = wgrad_out[:, part] * factor[0:1, 0:1]

    for q in sends:
        q.wait_send()
    z_sent(1)
    for h in range(2):
        ht_sent(h)


def on_device(hidden, targets, loss_mask, master, first_moment, second_moment):
    n_vocab, n_dp = lax.axis_size("vocab"), lax.axis_size("dp")
    n_o, n_y = n_vocab // 2, n_dp // 2
    toks, blk = hidden.shape
    rows, feats = master.shape
    group = 2 * n_dp * rows
    mid = group // 2
    vmem = pl.BlockSpec(memory_space=pltpu.VMEM)
    dma = pltpu.SemaphoreType.DMA
    arrays = [
        ((rows, feats), F32),
        ((2, n_o, toks // 2, blk), F32),
        ((n_o, group, blk), BF16),
        ((n_o, rows, blk), BF16),
        ((n_o, toks, blk), BF16),
        ((2, group, toks // 2), F32),
        ((2, group, toks // 2), F32),
        ((group, toks), BF16),
        ((group, toks), BF16),
        ((toks, group), BF16),
        ((2, n_o, toks // 2, blk), BF16),
        ((2, n_o + 1, toks // 2, blk), BF16),
        ((n_o, mid, blk), BF16),
        ((n_o, mid, blk), BF16),
        ((n_o, mid, blk), F32),
        ((n_y - 1, 2, n_o, rows, blk), BF16),
        ((n_y - 1, 2, n_o, rows, blk), BF16),
        ((n_o, rows, blk), BF16),
        ((n_o, rows, blk), BF16),
        ((2, n_o, 8, toks // 2), F32),
        ((n_dp, 8, 128), F32),
        ((n_dp, 16, 128), F32),
        ((n_vocab, 8, 128), F32),
    ]
    hidden_grad, clipped, scal = pl.pallas_call(
        functools.partial(kernel, n_vocab, n_dp),
        out_shape=(
            jax.ShapeDtypeStruct((toks, blk), BF16),
            jax.ShapeDtypeStruct((rows, feats), F32),
            jax.ShapeDtypeStruct((1, 1), F32),
        ),
        in_specs=[pl.BlockSpec(memory_space=pl.ANY)] * 2 + [vmem] * 2,
        out_specs=(vmem, vmem, vmem),
        scratch_shapes=[pltpu.VMEM(shape, dtype) for shape, dtype in arrays] + [
            dma((2,)), dma((2, 2, n_o)), dma((2, n_o)),
            dma((1,)), dma((n_y - 1, 2)), dma((n_y, 2)), dma((2 * n_dp,)),
            dma((2,)), dma((2,)),
            dma((2, n_o)), dma((2, n_o)),
            dma((2, n_o)), dma((2, n_o + 1)),
            dma((n_o,)), dma((n_o,)),
            dma((n_y - 1, 2, n_o)), dma((n_y - 1, 2, n_o)),
            dma((n_o,)), dma((n_o,)),
            dma((n_dp,)), dma((n_dp,)),
            dma((n_dp,)), dma((n_dp,)),
            dma((n_vocab,)), dma((n_vocab,)),
        ],
        compiler_params=pltpu.CompilerParams(
            collective_id=0, has_side_effects=True, vmem_limit_bytes=60 * 1024 * 1024
        ),
        name="head",
    )(hidden, master, targets.reshape(1, toks), loss_mask.reshape(1, toks))
    loss_value = scal.reshape(())
    new_first = beta_one * first_moment + (1.0 - beta_one) * clipped
    new_second = beta_two * second_moment + (1.0 - beta_two) * clipped * clipped
    first_scale = learn_rate / (1.0 - beta_one**STEP)
    second_scale = 1.0 / (1.0 - beta_two**STEP)
    new_master = master * (1.0 - learn_rate * decay_rate) - first_scale * new_first / (
        jnp.sqrt(second_scale * new_second) + epsilon_adam
    )
    return (loss_value, hidden_grad, new_master, new_first, new_second)


def solution(mesh):
    placed = (
        P("dp", "vocab"),
        P("dp"),
        P("dp"),
        P(("vocab", "dp"), None),
        P(("vocab", "dp"), None),
        P(("vocab", "dp"), None),
    )
    return jax.shard_map(
        on_device,
        mesh=mesh,
        in_specs=placed,
        out_specs=(
            P(),
            P("dp", "vocab"),
            P(("vocab", "dp"), None),
            P(("vocab", "dp"), None),
            P(("vocab", "dp"), None),
        ),
        check_vma=False,
    )
```

```python
import functools

import jax
import jax.numpy as jnp
from jax import lax
from jax.experimental import pallas as pl
from jax.experimental.pallas import tpu as pltpu
from jax.sharding import PartitionSpec as P

STEP = 10

beta_one = 0.9
beta_two = 0.95
learn_rate = 0.0003
decay_rate = 0.1
epsilon_adam = 1e-08
clip_norm = 1.0

MESH = pl.DeviceIdType.MESH
F32 = jnp.float32
BF16 = jnp.bfloat16


def kernel(
    n_vocab, n_dp,
    hid, master_hbm, targets, mask,
    hgrad_out, wgrad_out, scal_out,
    master, hterm, Wg, wsend, Hg, acc, lrecv, gt, gtp, g_tv,
    hsend, hrecv, gsend, grecv, gown, ysend, yrecv, xsend, xrecv,
    stat, cnt, sqa, sqb,
    in_sem, z_send, z_recv, wx_send, wy_send, ws_send, w_recv,
    l_send, l_recv, st_send, st_recv, ht_send, ht_recv,
    g_send, g_recv, y_send, y_recv, x_send, x_recv,
    c_send, c_recv, a_send, a_recv, b_send, b_recv,
):
    n_o = n_vocab // 2
    n_y = n_dp // 2
    v = lax.axis_index("vocab")
    r = lax.axis_index("dp")
    o = v // 2
    i = v % 2
    y = r // 2
    c = r % 2
    rows = master.shape[0]
    blk = hid.shape[1]
    toks = hid.shape[0]
    group = 2 * n_dp * rows
    th = toks // 2
    x_peer = (o * 2 + 1 - i, r)
    sibling = (v, y * 2 + 1 - c)

    def y_at(dy):
        return lax.rem(y + dy, n_y)

    def y_peer(dy):
        return (v, y_at(dy) * 2 + c)

    def rcopy(src, dst, ssem, rsem, dev):
        return pltpu.make_async_remote_copy(
            src_ref=src, dst_ref=dst, send_sem=ssem, recv_sem=rsem,
            device_id=dev, device_id_type=MESH,
        )

    load_master = pltpu.make_async_copy(master_hbm, master, in_sem.at[0])
    load_master.start()
    load_hid = pltpu.make_async_copy(hid, Hg.at[o], in_sem.at[1])
    load_hid.start()
    barrier = pltpu.get_barrier_semaphore()
    for k in range(1, n_vocab):
        pl.semaphore_signal(barrier, inc=1, device_id=(lax.rem(v + k, n_vocab), r), device_id_type=MESH)
    for k in range(1, n_dp):
        pl.semaphore_signal(barrier, inc=1, device_id=(v, lax.rem(r + k, n_dp)), device_id_type=MESH)
    pl.semaphore_wait(barrier, n_vocab - 1 + n_dp - 1)

    sends = []

    def z_copy(src, h, b, side):
        peer = o + 1 if side == 0 else o - 1
        part = pl.ds(h * th, th)
        src = src.at[part] if src is hid else src.at[b, part]
        return rcopy(src, Hg.at[b, part], z_send.at[side, h, b], z_recv.at[h, b], (peer * 2 + i, r))

    def z_own(h):
        @pl.when(o < n_o - 1)
        def _():
            z_copy(hid, h, o, 0).start()

        @pl.when(o > 0)
        def _():
            z_copy(hid, h, o, 1).start()

    def z_sent(h):
        @pl.when(o < n_o - 1)
        def _():
            z_copy(hid, h, o, 0).wait_send()

        @pl.when(o > 0)
        def _():
            z_copy(hid, h, o, 1).wait_send()

        for d in range(1, n_o):
            @pl.when((o - d >= 0) & (o < n_o - 1))
            def _():
                z_copy(Hg, h, o - d, 0).wait_send()

            @pl.when((o + d < n_o) & (o > 0))
            def _():
                z_copy(Hg, h, o + d, 1).wait_send()

    z_own(0)

    def z_step(h, d):
        @pl.when(o - d >= 0)
        def _():
            b = o - d
            z_copy(Hg, h, b, 0).wait_recv()

            @pl.when(o < n_o - 1)
            def _():
                z_copy(Hg, h, b, 0).start()

        @pl.when(o + d < n_o)
        def _():
            b = o + d
            z_copy(Hg, h, b, 1).wait_recv()

            @pl.when(o > 0)
            def _():
                z_copy(Hg, h, b, 1).start()

    def slot(ii, rr):
        return pl.ds(pl.multiple_of((ii * n_dp + rr) * rows, rows), rows)

    def w_slot(ii, rr):
        return Wg.at[:, slot(ii, rr), :]

    def w_sem(ii, rr):
        return w_recv.at[ii * n_dp + rr]

    def w_y(dy, k, ii):
        return rcopy(w_slot(ii, r), w_slot(ii, r), wy_send.at[dy - 1, k], w_sem(ii, r), y_peer(dy))

    def w_s(dy, k, ii):
        rr = y_at(dy) * 2 + c
        return rcopy(w_slot(ii, rr), w_slot(ii, rr), ws_send.at[dy, k], w_sem(ii, rr), sibling)

    def w_wait(ii, rr):
        rcopy(w_slot(ii, rr), w_slot(ii, rr), wx_send.at[0], w_sem(ii, rr), x_peer).wait_recv()

    load_master.wait()
    for b in range(n_o):
        cols = pl.ds(pl.multiple_of((2 * b + 1 - i) * blk, blk), blk)
        wsend[b] = master[:, cols].astype(BF16)
    wx = rcopy(wsend, w_slot(i, r), wx_send.at[0], w_sem(i, r), x_peer)
    wx.start()
    sends.append(wx)
    for b in range(n_o):
        cols = pl.ds(pl.multiple_of((2 * b + i) * blk, blk), blk)
        Wg[b, slot(i, r), :] = master[:, cols].astype(BF16)
    for dy in range(1, n_y):
        q = w_y(dy, 0, i)
        q.start()
        sends.append(q)
    q = w_s(0, 0, i)
    q.start()
    sends.append(q)

    maskf = mask[...].astype(F32)
    cnt[r] = jnp.broadcast_to(jnp.sum(maskf, axis=1, keepdims=True), cnt.shape[1:])
    for k in range(1, n_dp):
        q = rcopy(cnt.at[r], cnt.at[r], c_send.at[k], c_recv.at[r], (v, lax.rem(r + k, n_dp)))
        q.start()
        sends.append(q)
    load_hid.wait()

    steps = [(h, d) for h in range(2) for d in range(1, n_o)]
    done = [0]

    def z_until(n):
        while done[0] < min(n, len(steps)):
            z_step(*steps[done[0]])
            done[0] += 1

    z_until(2)
    w_wait(1 - i, r)
    for dy in range(1, n_y):
        q = w_y(dy, 1, 1 - i)
        q.start()
        sends.append(q)
    q = w_s(0, 1, 1 - i)
    q.start()
    sends.append(q)
    for dy in range(1, n_y):
        w_wait(i, y_at(dy) * 2 + c)
        q = w_s(dy, 0, i)
        q.start()
        sends.append(q)
    z_until(n_o - 1)
    z_sent(0)
    z_own(1)
    z_until(n_o)
    for dy in range(1, n_y):
        w_wait(1 - i, y_at(dy) * 2 + c)
        q = w_s(dy, 1, 1 - i)
        q.start()
        sends.append(q)
    for dy in range(n_y):
        for ii in range(2):
            w_wait(ii, y_at(dy) * 2 + 1 - c)

    def logits_of(h):
        part = slice(h * th, (h + 1) * th)
        total = None
        for b in range(n_o):
            term = lax.dot_general(
                Wg[b], Hg[b, part, :], (((1,), (1,)), ((), ())), preferred_element_type=F32
            )
            total = term if total is None else total + term
        acc[h] = total
        q = rcopy(acc.at[h], lrecv.at[h], l_send.at[h], l_recv.at[h], x_peer)
        q.start()
        return q

    def softmax_start(h, q):
        q.wait()
        part = slice(h * th, (h + 1) * th)
        logits = acc[h] + lrecv[h]
        acc[h] = logits
        ids = targets[:, part] - o * group
        hot = lax.broadcasted_iota(jnp.int32, (group, th), 0) == ids
        top = jnp.max(logits, axis=0, keepdims=True)
        stat[h, o] = jnp.zeros(stat.shape[2:], F32)
        stat[h, o, 0:1, :] = top
        stat[h, o, 1:2, :] = jnp.sum(jnp.exp(logits - top), axis=0, keepdims=True)
        stat[h, o, 2:3, :] = jnp.sum(jnp.where(hot, logits, 0.0), axis=0, keepdims=True)
        for k in range(1, n_o):
            dev = (lax.rem(o + k, n_o) * 2 + i, r)
            q = rcopy(stat.at[h, o], stat.at[h, o], st_send.at[h, k], st_recv.at[h, o], dev)
            q.start()
            sends.append(q)

    def softmax_end(h):
        part = slice(h * th, (h + 1) * th)
        for k in range(1, n_o):
            b = lax.rem(o + k, n_o)
            rcopy(stat.at[h, b], stat.at[h, b], st_send.at[h, k], st_recv.at[h, b], x_peer).wait_recv()
        row_top = stat[h, 0, 0:1, :]
        for b in range(1, n_o):
            row_top = jnp.maximum(row_top, stat[h, b, 0:1, :])
        exp_sum = jnp.zeros_like(row_top)
        picked = jnp.zeros_like(row_top)
        for b in range(n_o):
            exp_sum += stat[h, b, 1:2, :] * jnp.exp(stat[h, b, 0:1, :] - row_top)
            picked += stat[h, b, 2:3, :]
        log_norm = row_top + jnp.log(exp_sum)
        ids = targets[:, part] - o * group
        hot = (lax.broadcasted_iota(jnp.int32, (group, th), 0) == ids).astype(F32)
        grad = maskf[:, part] * (jnp.exp(acc[h] - log_norm) - hot)
        gt[:, part] = grad.astype(BF16)
        g_tv[part, :] = grad.T.astype(BF16)
        return jnp.sum(maskf[:, part] * (log_norm - picked), axis=1, keepdims=True)

    def hidden_terms(h, ks):
        part = slice(h * th, (h + 1) * th)
        for k in ks:
            b = jnp.where(o < n_o // 2, n_o - 1 - k, k)
            hterm[h, b] = jnp.dot(g_tv[part, :], Wg[b], preferred_element_type=F32)

    def ht_copy(h, b, side):
        if side == 0:
            to, at = o + 1, b
        else:
            to, at = o - 1, jnp.where(b == o - 1, n_o, b)
        return rcopy(hsend.at[h, b], hrecv.at[h, at], ht_send.at[h, b], ht_recv.at[h, at], (to * 2 + i, r))

    def ht_wait(h, at):
        rcopy(hsend.at[h, 0], hrecv.at[h, at], ht_send.at[h, 0], ht_recv.at[h, at], x_peer).wait_recv()

    def ht_step(h, s):
        for side in range(2):
            place = o if side == 0 else n_o - 1 - o
            b = n_o - s + o if side == 0 else s - 1 - place

            @pl.when(place < s)
            def _():
                @pl.when(place + 1 < s)
                def _():
                    ht_copy(h, b + 1 if side == 0 else b - 1, side).wait_send()

                @pl.when(place > 0)
                def _():
                    ht_wait(h, b)
                    hsend[h, b] = (hterm[h, b] + hrecv[h, b].astype(F32)).astype(BF16)

                @pl.when(place == 0)
                def _():
                    hsend[h, b] = hterm[h, b].astype(BF16)

                ht_copy(h, b, side).start()

    def ht_finish(h):
        @pl.when(o > 0)
        def _():
            ht_wait(h, o)
            hterm[h, o] = hterm[h, o] + hrecv[h, o].astype(F32)

        @pl.when(o < n_o - 1)
        def _():
            ht_wait(h, n_o)
            hterm[h, o] = hterm[h, o] + hrecv[h, n_o].astype(F32)

    def ht_sent(h):
        for side in range(2):
            place = o if side == 0 else n_o - 1 - o

            @pl.when(place < n_o - 1)
            def _():
                ht_copy(h, o + 1 if side == 0 else o - 1, side).wait_send()

    ht_steps = [(h, s) for h in range(2) for s in range(1, n_o)]
    ht_done = [0]

    def ht_until(n):
        while ht_done[0] < min(n, len(ht_steps)):
            ht_step(*ht_steps[ht_done[0]])
            ht_done[0] += 1

    q0 = logits_of(0)
    z_until(len(steps) - 1)
    softmax_start(0, q0)
    z_until(len(steps))
    q1 = logits_of(1)
    loss_local = softmax_end(0)
    hidden_terms(0, [0])
    ht_until(1)
    hidden_terms(0, range(1, n_o))
    softmax_start(1, q1)
    loss_local = loss_local + softmax_end(1)

    m = 0
    for cc in (1 - c, c):
        for dy in list(range(1, n_y)) + [0]:
            for ii in (1 - i, i):
                gtp[m * rows:(m + 1) * rows, :] = gt[slot(ii, y_at(dy) * 2 + cc), :]
                m += 1
    mid = group // 2
    for b in range(n_o):
        gsend[b] = jnp.dot(gtp[:mid, :], Hg[b], preferred_element_type=F32).astype(BF16)
        q = rcopy(gsend.at[b], grecv.at[b], g_send.at[b], g_recv.at[b], sibling)
        q.start()
        sends.append(q)
    ht_until(2)
    for b in range(n_o):
        gown[b] = jnp.dot(gtp[mid:, :], Hg[b], preferred_element_type=F32)
    def y_copy(dy, ii, b):
        return rcopy(
            ysend.at[dy - 1, ii, b], yrecv.at[dy - 1, ii, b],
            y_send.at[dy - 1, ii, b], y_recv.at[dy - 1, ii, b], y_peer(dy),
        )

    def two_cores(dy, ii, b):
        at = ((dy - 1) * 2 + ii) * rows
        return gown[b, at:at + rows, :] + grecv[b, at:at + rows, :].astype(F32)

    def y_start(dy, ii, b):
        ysend[dy - 1, ii, b] = two_cores(dy, ii, b).astype(BF16)
        q = y_copy(dy, ii, b)
        q.start()
        sends.append(q)

    for b in range(n_o):
        rcopy(gsend.at[b], grecv.at[b], g_send.at[b], g_recv.at[b], sibling).wait_recv()
        for dy in range(1, n_y):
            y_start(dy, 0, b)
    hidden_terms(1, range(n_o))
    ht_until(n_o)
    squares = jnp.zeros((8, blk), F32)
    for b in range(n_o):
        total = two_cores(n_y, 0, b)
        for dy in range(1, n_y):
            y_copy(dy, 0, b).wait_recv()
            y_start(dy, 1, b)
            total += yrecv[dy - 1, 0, b].astype(F32)
        if b == n_o // 2:
            ht_until(n_o + 1)
        xsend[b] = total.astype(BF16)
        q = rcopy(xsend.at[b], xrecv.at[b], x_send.at[b], x_recv.at[b], x_peer)
        q.start()
        sends.append(q)
    ht_until(len(ht_steps))
    for b in range(n_o):
        mine = two_cores(n_y, 1, b)
        for dy in range(1, n_y):
            y_copy(dy, 1, b).wait_recv()
            mine += yrecv[dy - 1, 1, b].astype(F32)
        wgrad_out[:, pl.ds(pl.multiple_of((2 * b + i) * blk, blk), blk)] = mine
        squares += jnp.sum((mine * mine).reshape(rows // 8, 8, blk), axis=0)
    for b in range(n_o):
        rcopy(xsend.at[b], xrecv.at[b], x_send.at[b], x_recv.at[b], x_peer).wait_recv()
        theirs = xrecv[b].astype(F32)
        wgrad_out[:, pl.ds(pl.multiple_of((2 * b + 1 - i) * blk, blk), blk)] = theirs
        squares += jnp.sum((theirs * theirs).reshape(rows // 8, 8, blk), axis=0)
    square = jnp.sum(jnp.sum(squares, axis=0, keepdims=True), axis=1, keepdims=True)

    sqa[r, 0:8, :] = jnp.broadcast_to(square, (8, 128))
    sqa[r, 8:16, :] = jnp.broadcast_to(loss_local, (8, 128))
    for k in range(1, n_dp):
        q = rcopy(sqa.at[r], sqa.at[r], a_send.at[k], a_recv.at[r], (v, lax.rem(r + k, n_dp)))
        q.start()
        sends.append(q)
    for k in range(1, n_dp):
        b = lax.rem(r + k, n_dp)
        rcopy(sqa.at[b], sqa.at[b], a_send.at[k], a_recv.at[b], x_peer).wait_recv()
        rcopy(cnt.at[b], cnt.at[b], c_send.at[k], c_recv.at[b], x_peer).wait_recv()
    both = sqa[0]
    count = cnt[0]
    for b in range(1, n_dp):
        both = both + sqa[b]
        count = count + cnt[b]
    sqb[v] = both[0:8]
    for k in range(1, n_vocab):
        q = rcopy(sqb.at[v], sqb.at[v], b_send.at[k], b_recv.at[v], (lax.rem(v + k, n_vocab), r))
        q.start()
        sends.append(q)

    for h in range(2):
        part = slice(h * th, (h + 1) * th)
        ht_finish(h)
        hgrad_out[part, :] = (hterm[h, o] / count[0:1, 0:1]).astype(BF16)

    for k in range(1, n_vocab):
        b = lax.rem(v + k, n_vocab)
        rcopy(sqb.at[b], sqb.at[b], b_send.at[k], b_recv.at[b], x_peer).wait_recv()
    square_sum = sqb[0]
    for b in range(1, n_vocab):
        square_sum = square_sum + sqb[b]
    norm = jnp.sqrt(square_sum) / count
    factor = jnp.minimum(1.0, clip_norm / (norm + 1e-06)) / count
    scal_out[...] = (both[8:16] / count)[0:1, 0:1]
    for b in range(n_vocab):
        part = slice(b * blk, (b + 1) * blk)
        wgrad_out[:, part] = wgrad_out[:, part] * factor[0:1, 0:1]

    for q in sends:
        q.wait_send()
    z_sent(1)
    for h in range(2):
        ht_sent(h)


def update(clipped_ref, master_ref, first_ref, second_ref, new_master, new_first, new_second):
    first_scale = learn_rate / (1.0 - beta_one**STEP)
    second_scale = 1.0 / (1.0 - beta_two**STEP)
    clipped = clipped_ref[...]
    first = beta_one * first_ref[...] + (1.0 - beta_one) * clipped
    second = beta_two * second_ref[...] + (1.0 - beta_two) * clipped * clipped
    new_first[...] = first
    new_second[...] = second
    scaled = second_scale * second
    below = scaled * lax.rsqrt(scaled) + epsilon_adam
    inverse = pl.reciprocal(below, approx=True)
    inverse = inverse * (2.0 - below * inverse)
    new_master[...] = master_ref[...] * (1.0 - learn_rate * decay_rate) - first_scale * first * inverse


def on_device(hidden, targets, loss_mask, master, first_moment, second_moment):
    n_vocab, n_dp = lax.axis_size("vocab"), lax.axis_size("dp")
    n_o, n_y = n_vocab // 2, n_dp // 2
    toks, blk = hidden.shape
    rows, feats = master.shape
    group = 2 * n_dp * rows
    mid = group // 2
    vmem = pl.BlockSpec(memory_space=pltpu.VMEM)
    dma = pltpu.SemaphoreType.DMA
    arrays = [
        ((rows, feats), F32),
        ((2, n_o, toks // 2, blk), F32),
        ((n_o, group, blk), BF16),
        ((n_o, rows, blk), BF16),
        ((n_o, toks, blk), BF16),
        ((2, group, toks // 2), F32),
        ((2, group, toks // 2), F32),
        ((group, toks), BF16),
        ((group, toks), BF16),
        ((toks, group), BF16),
        ((2, n_o, toks // 2, blk), BF16),
        ((2, n_o + 1, toks // 2, blk), BF16),
        ((n_o, mid, blk), BF16),
        ((n_o, mid, blk), BF16),
        ((n_o, mid, blk), F32),
        ((n_y - 1, 2, n_o, rows, blk), BF16),
        ((n_y - 1, 2, n_o, rows, blk), BF16),
        ((n_o, rows, blk), BF16),
        ((n_o, rows, blk), BF16),
        ((2, n_o, 8, toks // 2), F32),
        ((n_dp, 8, 128), F32),
        ((n_dp, 16, 128), F32),
        ((n_vocab, 8, 128), F32),
    ]
    hidden_grad, clipped, scal = pl.pallas_call(
        functools.partial(kernel, n_vocab, n_dp),
        out_shape=(
            jax.ShapeDtypeStruct((toks, blk), BF16),
            jax.ShapeDtypeStruct((rows, feats), F32),
            jax.ShapeDtypeStruct((1, 1), F32),
        ),
        in_specs=[pl.BlockSpec(memory_space=pl.ANY)] * 2 + [vmem] * 2,
        out_specs=(vmem, vmem, vmem),
        scratch_shapes=[pltpu.VMEM(shape, dtype) for shape, dtype in arrays] + [
            dma((2,)), dma((2, 2, n_o)), dma((2, n_o)),
            dma((1,)), dma((n_y - 1, 2)), dma((n_y, 2)), dma((2 * n_dp,)),
            dma((2,)), dma((2,)),
            dma((2, n_o)), dma((2, n_o)),
            dma((2, n_o)), dma((2, n_o + 1)),
            dma((n_o,)), dma((n_o,)),
            dma((n_y - 1, 2, n_o)), dma((n_y - 1, 2, n_o)),
            dma((n_o,)), dma((n_o,)),
            dma((n_dp,)), dma((n_dp,)),
            dma((n_dp,)), dma((n_dp,)),
            dma((n_vocab,)), dma((n_vocab,)),
        ],
        compiler_params=pltpu.CompilerParams(
            collective_id=0, has_side_effects=True, vmem_limit_bytes=60 * 1024 * 1024
        ),
        name="head",
    )(hidden, master, targets.reshape(1, toks), loss_mask.reshape(1, toks))
    loss_value = scal.reshape(())
    wide = feats // 8
    block = pl.BlockSpec((rows, wide), lambda j: (0, j))
    new_master, new_first, new_second = pl.pallas_call(
        update,
        grid=(feats // wide,),
        out_shape=(jax.ShapeDtypeStruct((rows, feats), F32),) * 3,
        in_specs=[block] * 4,
        out_specs=(block,) * 3,
        compiler_params=pltpu.CompilerParams(vmem_limit_bytes=16 * 1024 * 1024),
        name="update",
    )(clipped, master, first_moment, second_moment)
    return (loss_value, hidden_grad, new_master, new_first, new_second)


def solution(mesh):
    placed = (
        P("dp", "vocab"),
        P("dp"),
        P("dp"),
        P(("vocab", "dp"), None),
        P(("vocab", "dp"), None),
        P(("vocab", "dp"), None),
    )
    return jax.shard_map(
        on_device,
        mesh=mesh,
        in_specs=placed,
        out_specs=(
            P(),
            P("dp", "vocab"),
            P(("vocab", "dp"), None),
            P(("vocab", "dp"), None),
            P(("vocab", "dp"), None),
        ),
        check_vma=False,
    )
```

```python
import functools

import jax
import jax.numpy as jnp
from jax import lax
from jax.experimental import pallas as pl
from jax.experimental.pallas import tpu as pltpu
from jax.sharding import PartitionSpec as P

STEP = 10

beta_one = 0.9
beta_two = 0.95
learn_rate = 0.0003
decay_rate = 0.1
epsilon_adam = 1e-08
clip_norm = 1.0

MESH = pl.DeviceIdType.MESH
F32 = jnp.float32
BF16 = jnp.bfloat16


def kernel(
    n_vocab, n_dp,
    hid, master_hbm, targets, mask,
    hgrad_out, wgrad_out, scal_out,
    master, hterm, Wg, wsend, Hg, acc, lrecv, gt, gtp, g_tv,
    hsend, hrecv, gsend, grecv, gown, ysend, yrecv, xsend, xrecv,
    stat, cnt, sqa, sqb,
    in_sem, z_send, z_recv, wx_send, wy_send, ws_send, w_recv,
    l_send, l_recv, st_send, st_recv, ht_send, ht_recv,
    g_send, g_recv, y_send, y_recv, x_send, x_recv,
    c_send, c_recv, a_send, a_recv, b_send, b_recv,
):
    n_o = n_vocab // 2
    n_y = n_dp // 2
    v = lax.axis_index("vocab")
    r = lax.axis_index("dp")
    o = v // 2
    i = v % 2
    y = r // 2
    c = r % 2
    rows = master.shape[0]
    blk = hid.shape[1]
    toks = hid.shape[0]
    group = 2 * n_dp * rows
    th = toks // 2
    x_peer = (o * 2 + 1 - i, r)
    sibling = (v, y * 2 + 1 - c)

    def y_at(dy):
        return lax.rem(y + dy, n_y)

    def y_peer(dy):
        return (v, y_at(dy) * 2 + c)

    def rcopy(src, dst, ssem, rsem, dev):
        return pltpu.make_async_remote_copy(
            src_ref=src, dst_ref=dst, send_sem=ssem, recv_sem=rsem,
            device_id=dev, device_id_type=MESH,
        )

    load_master = pltpu.make_async_copy(master_hbm, master, in_sem.at[0])
    load_master.start()
    load_hid = pltpu.make_async_copy(hid, Hg.at[o], in_sem.at[1])
    load_hid.start()
    barrier = pltpu.get_barrier_semaphore()
    for k in range(1, n_vocab):
        pl.semaphore_signal(barrier, inc=1, device_id=(lax.rem(v + k, n_vocab), r), device_id_type=MESH)
    for k in range(1, n_dp):
        pl.semaphore_signal(barrier, inc=1, device_id=(v, lax.rem(r + k, n_dp)), device_id_type=MESH)
    pl.semaphore_wait(barrier, n_vocab - 1 + n_dp - 1)

    sends = []

    def z_copy(src, h, b, side):
        peer = o + 1 if side == 0 else o - 1
        part = pl.ds(h * th, th)
        src = src.at[part] if src is hid else src.at[b, part]
        return rcopy(src, Hg.at[b, part], z_send.at[side, h, b], z_recv.at[h, b], (peer * 2 + i, r))

    def z_own(h):
        @pl.when(o < n_o - 1)
        def _():
            z_copy(hid, h, o, 0).start()

        @pl.when(o > 0)
        def _():
            z_copy(hid, h, o, 1).start()

    def z_sent(h):
        @pl.when(o < n_o - 1)
        def _():
            z_copy(hid, h, o, 0).wait_send()

        @pl.when(o > 0)
        def _():
            z_copy(hid, h, o, 1).wait_send()

        for d in range(1, n_o):
            @pl.when((o - d >= 0) & (o < n_o - 1))
            def _():
                z_copy(Hg, h, o - d, 0).wait_send()

            @pl.when((o + d < n_o) & (o > 0))
            def _():
                z_copy(Hg, h, o + d, 1).wait_send()

    z_own(0)

    def z_step(h, d):
        @pl.when(o - d >= 0)
        def _():
            b = o - d
            z_copy(Hg, h, b, 0).wait_recv()

            @pl.when(o < n_o - 1)
            def _():
                z_copy(Hg, h, b, 0).start()

        @pl.when(o + d < n_o)
        def _():
            b = o + d
            z_copy(Hg, h, b, 1).wait_recv()

            @pl.when(o > 0)
            def _():
                z_copy(Hg, h, b, 1).start()

    def slot(ii, rr):
        return pl.ds(pl.multiple_of((ii * n_dp + rr) * rows, rows), rows)

    def w_slot(ii, rr):
        return Wg.at[:, slot(ii, rr), :]

    def w_sem(ii, rr):
        return w_recv.at[ii * n_dp + rr]

    def w_y(dy, k, ii):
        return rcopy(w_slot(ii, r), w_slot(ii, r), wy_send.at[dy - 1, k], w_sem(ii, r), y_peer(dy))

    def w_s(dy, k, ii):
        rr = y_at(dy) * 2 + c
        return rcopy(w_slot(ii, rr), w_slot(ii, rr), ws_send.at[dy, k], w_sem(ii, rr), sibling)

    def w_wait(ii, rr):
        rcopy(w_slot(ii, rr), w_slot(ii, rr), wx_send.at[0], w_sem(ii, rr), x_peer).wait_recv()

    load_master.wait()
    for b in range(n_o):
        cols = pl.ds(pl.multiple_of((2 * b + 1 - i) * blk, blk), blk)
        wsend[b] = master[:, cols].astype(BF16)
    wx = rcopy(wsend, w_slot(i, r), wx_send.at[0], w_sem(i, r), x_peer)
    wx.start()
    sends.append(wx)
    for b in range(n_o):
        cols = pl.ds(pl.multiple_of((2 * b + i) * blk, blk), blk)
        Wg[b, slot(i, r), :] = master[:, cols].astype(BF16)
    for dy in range(1, n_y):
        q = w_y(dy, 0, i)
        q.start()
        sends.append(q)
    q = w_s(0, 0, i)
    q.start()
    sends.append(q)

    maskf = mask[...].astype(F32)
    cnt[r] = jnp.broadcast_to(jnp.sum(maskf, axis=1, keepdims=True), cnt.shape[1:])
    for k in range(1, n_dp):
        q = rcopy(cnt.at[r], cnt.at[r], c_send.at[k], c_recv.at[r], (v, lax.rem(r + k, n_dp)))
        q.start()
        sends.append(q)
    load_hid.wait()

    steps = [(h, d) for h in range(2) for d in range(1, n_o)]
    done = [0]

    def z_until(n):
        while done[0] < min(n, len(steps)):
            z_step(*steps[done[0]])
            done[0] += 1

    z_until(2)
    w_wait(1 - i, r)
    for dy in range(1, n_y):
        q = w_y(dy, 1, 1 - i)
        q.start()
        sends.append(q)
    q = w_s(0, 1, 1 - i)
    q.start()
    sends.append(q)
    for dy in range(1, n_y):
        w_wait(i, y_at(dy) * 2 + c)
        q = w_s(dy, 0, i)
        q.start()
        sends.append(q)
    z_until(n_o - 1)
    z_sent(0)
    z_own(1)
    z_until(n_o)
    for dy in range(1, n_y):
        w_wait(1 - i, y_at(dy) * 2 + c)
        q = w_s(dy, 1, 1 - i)
        q.start()
        sends.append(q)
    for dy in range(n_y):
        for ii in range(2):
            w_wait(ii, y_at(dy) * 2 + 1 - c)

    def logits_of(h):
        part = slice(h * th, (h + 1) * th)
        total = None
        for b in range(n_o):
            term = lax.dot_general(
                Wg[b], Hg[b, part, :], (((1,), (1,)), ((), ())), preferred_element_type=F32
            )
            total = term if total is None else total + term
        acc[h] = total
        q = rcopy(acc.at[h], lrecv.at[h], l_send.at[h], l_recv.at[h], x_peer)
        q.start()
        return q

    def softmax_start(h, q):
        q.wait()
        part = slice(h * th, (h + 1) * th)
        logits = acc[h] + lrecv[h]
        acc[h] = logits
        ids = targets[:, part] - o * group
        hot = lax.broadcasted_iota(jnp.int32, (group, th), 0) == ids
        top = jnp.max(logits, axis=0, keepdims=True)
        stat[h, o] = jnp.zeros(stat.shape[2:], F32)
        stat[h, o, 0:1, :] = top
        stat[h, o, 1:2, :] = jnp.sum(jnp.exp(logits - top), axis=0, keepdims=True)
        stat[h, o, 2:3, :] = jnp.sum(jnp.where(hot, logits, 0.0), axis=0, keepdims=True)
        for k in range(1, n_o):
            dev = (lax.rem(o + k, n_o) * 2 + i, r)
            q = rcopy(stat.at[h, o], stat.at[h, o], st_send.at[h, k], st_recv.at[h, o], dev)
            q.start()
            sends.append(q)

    def softmax_end(h):
        part = slice(h * th, (h + 1) * th)
        for k in range(1, n_o):
            b = lax.rem(o + k, n_o)
            rcopy(stat.at[h, b], stat.at[h, b], st_send.at[h, k], st_recv.at[h, b], x_peer).wait_recv()
        row_top = stat[h, 0, 0:1, :]
        for b in range(1, n_o):
            row_top = jnp.maximum(row_top, stat[h, b, 0:1, :])
        exp_sum = jnp.zeros_like(row_top)
        picked = jnp.zeros_like(row_top)
        for b in range(n_o):
            exp_sum += stat[h, b, 1:2, :] * jnp.exp(stat[h, b, 0:1, :] - row_top)
            picked += stat[h, b, 2:3, :]
        log_norm = row_top + jnp.log(exp_sum)
        ids = targets[:, part] - o * group
        hot = (lax.broadcasted_iota(jnp.int32, (group, th), 0) == ids).astype(F32)
        grad = maskf[:, part] * (jnp.exp(acc[h] - log_norm) - hot)
        gt[:, part] = grad.astype(BF16)
        g_tv[part, :] = grad.T.astype(BF16)
        return jnp.sum(maskf[:, part] * (log_norm - picked), axis=1, keepdims=True)

    def hidden_terms(h, ks):
        part = slice(h * th, (h + 1) * th)
        for k in ks:
            b = jnp.where(o < n_o // 2, n_o - 1 - k, k)
            hterm[h, b] = jnp.dot(g_tv[part, :], Wg[b], preferred_element_type=F32)

    def ht_copy(h, b, side):
        if side == 0:
            to, at = o + 1, b
        else:
            to, at = o - 1, jnp.where(b == o - 1, n_o, b)
        return rcopy(hsend.at[h, b], hrecv.at[h, at], ht_send.at[h, b], ht_recv.at[h, at], (to * 2 + i, r))

    def ht_wait(h, at):
        rcopy(hsend.at[h, 0], hrecv.at[h, at], ht_send.at[h, 0], ht_recv.at[h, at], x_peer).wait_recv()

    def ht_step(h, s):
        for side in range(2):
            place = o if side == 0 else n_o - 1 - o
            b = n_o - s + o if side == 0 else s - 1 - place

            @pl.when(place < s)
            def _():
                @pl.when(place + 1 < s)
                def _():
                    ht_copy(h, b + 1 if side == 0 else b - 1, side).wait_send()

                @pl.when(place > 0)
                def _():
                    ht_wait(h, b)
                    hsend[h, b] = (hterm[h, b] + hrecv[h, b].astype(F32)).astype(BF16)

                @pl.when(place == 0)
                def _():
                    hsend[h, b] = hterm[h, b].astype(BF16)

                ht_copy(h, b, side).start()

    def ht_finish(h):
        @pl.when(o > 0)
        def _():
            ht_wait(h, o)
            hterm[h, o] = hterm[h, o] + hrecv[h, o].astype(F32)

        @pl.when(o < n_o - 1)
        def _():
            ht_wait(h, n_o)
            hterm[h, o] = hterm[h, o] + hrecv[h, n_o].astype(F32)

    def ht_sent(h):
        for side in range(2):
            place = o if side == 0 else n_o - 1 - o

            @pl.when(place < n_o - 1)
            def _():
                ht_copy(h, o + 1 if side == 0 else o - 1, side).wait_send()

    ht_steps = [(h, s) for h in range(2) for s in range(1, n_o)]
    ht_done = [0]

    def ht_until(n):
        while ht_done[0] < min(n, len(ht_steps)):
            ht_step(*ht_steps[ht_done[0]])
            ht_done[0] += 1

    q0 = logits_of(0)
    z_until(len(steps) - 1)
    softmax_start(0, q0)
    z_until(len(steps))
    q1 = logits_of(1)
    loss_local = softmax_end(0)
    hidden_terms(0, [0])
    ht_until(1)
    hidden_terms(0, range(1, n_o))
    softmax_start(1, q1)
    loss_local = loss_local + softmax_end(1)

    m = 0
    for cc in (1 - c, c):
        for dy in list(range(1, n_y)) + [0]:
            for ii in (1 - i, i):
                gtp[m * rows:(m + 1) * rows, :] = gt[slot(ii, y_at(dy) * 2 + cc), :]
                m += 1
    mid = group // 2
    for b in range(n_o):
        gsend[b] = jnp.dot(gtp[:mid, :], Hg[b], preferred_element_type=F32).astype(BF16)
        q = rcopy(gsend.at[b], grecv.at[b], g_send.at[b], g_recv.at[b], sibling)
        q.start()
        sends.append(q)
    ht_until(2)
    for b in range(n_o):
        gown[b] = jnp.dot(gtp[mid:, :], Hg[b], preferred_element_type=F32)
    def y_copy(dy, ii, b):
        return rcopy(
            ysend.at[dy - 1, ii, b], yrecv.at[dy - 1, ii, b],
            y_send.at[dy - 1, ii, b], y_recv.at[dy - 1, ii, b], y_peer(dy),
        )

    def two_cores(dy, ii, b):
        at = ((dy - 1) * 2 + ii) * rows
        return gown[b, at:at + rows, :] + grecv[b, at:at + rows, :].astype(F32)

    def y_start(dy, ii, b):
        ysend[dy - 1, ii, b] = two_cores(dy, ii, b).astype(BF16)
        q = y_copy(dy, ii, b)
        q.start()
        sends.append(q)

    for b in range(n_o):
        rcopy(gsend.at[b], grecv.at[b], g_send.at[b], g_recv.at[b], sibling).wait_recv()
        for dy in range(1, n_y):
            y_start(dy, 0, b)
    hidden_terms(1, range(n_o))
    ht_until(n_o)
    squares = jnp.zeros((8, blk), F32)
    for b in range(n_o):
        total = two_cores(n_y, 0, b)
        for dy in range(1, n_y):
            y_copy(dy, 0, b).wait_recv()
            y_start(dy, 1, b)
            total += yrecv[dy - 1, 0, b].astype(F32)
        if b == n_o // 2:
            ht_until(n_o + 1)
        xsend[b] = total.astype(BF16)
        q = rcopy(xsend.at[b], xrecv.at[b], x_send.at[b], x_recv.at[b], x_peer)
        q.start()
        sends.append(q)
    ht_until(len(ht_steps))
    for b in range(n_o):
        mine = two_cores(n_y, 1, b)
        for dy in range(1, n_y):
            y_copy(dy, 1, b).wait_recv()
            mine += yrecv[dy - 1, 1, b].astype(F32)
        wgrad_out[:, pl.ds(pl.multiple_of((2 * b + i) * blk, blk), blk)] = mine
        squares += jnp.sum((mine * mine).reshape(rows // 8, 8, blk), axis=0)
    for b in range(n_o):
        rcopy(xsend.at[b], xrecv.at[b], x_send.at[b], x_recv.at[b], x_peer).wait_recv()
        theirs = xrecv[b].astype(F32)
        wgrad_out[:, pl.ds(pl.multiple_of((2 * b + 1 - i) * blk, blk), blk)] = theirs
        squares += jnp.sum((theirs * theirs).reshape(rows // 8, 8, blk), axis=0)
    square = jnp.sum(jnp.sum(squares, axis=0, keepdims=True), axis=1, keepdims=True)

    sqa[r, 0:8, :] = jnp.broadcast_to(square, (8, 128))
    sqa[r, 8:16, :] = jnp.broadcast_to(loss_local, (8, 128))
    for k in range(1, n_dp):
        q = rcopy(sqa.at[r], sqa.at[r], a_send.at[k], a_recv.at[r], (v, lax.rem(r + k, n_dp)))
        q.start()
        sends.append(q)
    for k in range(1, n_dp):
        b = lax.rem(r + k, n_dp)
        rcopy(sqa.at[b], sqa.at[b], a_send.at[k], a_recv.at[b], x_peer).wait_recv()
        rcopy(cnt.at[b], cnt.at[b], c_send.at[k], c_recv.at[b], x_peer).wait_recv()
    both = sqa[0]
    count = cnt[0]
    for b in range(1, n_dp):
        both = both + sqa[b]
        count = count + cnt[b]
    sqb[v] = both[0:8]
    for k in range(1, n_vocab):
        q = rcopy(sqb.at[v], sqb.at[v], b_send.at[k], b_recv.at[v], (lax.rem(v + k, n_vocab), r))
        q.start()
        sends.append(q)

    for h in range(2):
        part = slice(h * th, (h + 1) * th)
        ht_finish(h)
        hgrad_out[part, :] = (hterm[h, o] / count[0:1, 0:1]).astype(BF16)

    for k in range(1, n_vocab):
        b = lax.rem(v + k, n_vocab)
        rcopy(sqb.at[b], sqb.at[b], b_send.at[k], b_recv.at[b], x_peer).wait_recv()
    square_sum = sqb[0]
    for b in range(1, n_vocab):
        square_sum = square_sum + sqb[b]
    norm = jnp.sqrt(square_sum) / count
    factor = jnp.minimum(1.0, clip_norm / (norm + 1e-06)) / count
    scal_out[...] = (both[8:16] / count)[0:1, 0:1]
    for b in range(n_vocab):
        part = slice(b * blk, (b + 1) * blk)
        wgrad_out[:, part] = wgrad_out[:, part] * factor[0:1, 0:1]

    for q in sends:
        q.wait_send()
    z_sent(1)
    for h in range(2):
        ht_sent(h)


def update(clipped_ref, master_ref, first_ref, second_ref, grad_ref, new_master, new_first, new_second, grad_out):
    grad_out[...] = grad_ref[...]
    first_scale = learn_rate / (1.0 - beta_one**STEP)
    second_scale = 1.0 / (1.0 - beta_two**STEP)
    clipped = clipped_ref[...]
    first = beta_one * first_ref[...] + (1.0 - beta_one) * clipped
    second = beta_two * second_ref[...] + (1.0 - beta_two) * clipped * clipped
    new_first[...] = first
    new_second[...] = second
    scaled = second_scale * second
    below = scaled * lax.rsqrt(scaled) + epsilon_adam
    inverse = pl.reciprocal(below, approx=True)
    inverse = inverse * (2.0 - below * inverse)
    new_master[...] = master_ref[...] * (1.0 - learn_rate * decay_rate) - first_scale * first * inverse


def on_device(hidden, targets, loss_mask, master, first_moment, second_moment):
    n_vocab, n_dp = lax.axis_size("vocab"), lax.axis_size("dp")
    n_o, n_y = n_vocab // 2, n_dp // 2
    toks, blk = hidden.shape
    rows, feats = master.shape
    group = 2 * n_dp * rows
    mid = group // 2
    vmem = pl.BlockSpec(memory_space=pltpu.VMEM)
    dma = pltpu.SemaphoreType.DMA
    arrays = [
        ((rows, feats), F32),
        ((2, n_o, toks // 2, blk), F32),
        ((n_o, group, blk), BF16),
        ((n_o, rows, blk), BF16),
        ((n_o, toks, blk), BF16),
        ((2, group, toks // 2), F32),
        ((2, group, toks // 2), F32),
        ((group, toks), BF16),
        ((group, toks), BF16),
        ((toks, group), BF16),
        ((2, n_o, toks // 2, blk), BF16),
        ((2, n_o + 1, toks // 2, blk), BF16),
        ((n_o, mid, blk), BF16),
        ((n_o, mid, blk), BF16),
        ((n_o, mid, blk), F32),
        ((n_y - 1, 2, n_o, rows, blk), BF16),
        ((n_y - 1, 2, n_o, rows, blk), BF16),
        ((n_o, rows, blk), BF16),
        ((n_o, rows, blk), BF16),
        ((2, n_o, 8, toks // 2), F32),
        ((n_dp, 8, 128), F32),
        ((n_dp, 16, 128), F32),
        ((n_vocab, 8, 128), F32),
    ]
    hidden_grad, clipped, scal = pl.pallas_call(
        functools.partial(kernel, n_vocab, n_dp),
        out_shape=(
            jax.ShapeDtypeStruct((toks, blk), BF16),
            jax.ShapeDtypeStruct((rows, feats), F32),
            jax.ShapeDtypeStruct((1, 1), F32),
        ),
        in_specs=[pl.BlockSpec(memory_space=pl.ANY)] * 2 + [vmem] * 2,
        out_specs=(vmem, vmem, vmem),
        scratch_shapes=[pltpu.VMEM(shape, dtype) for shape, dtype in arrays] + [
            dma((2,)), dma((2, 2, n_o)), dma((2, n_o)),
            dma((1,)), dma((n_y - 1, 2)), dma((n_y, 2)), dma((2 * n_dp,)),
            dma((2,)), dma((2,)),
            dma((2, n_o)), dma((2, n_o)),
            dma((2, n_o)), dma((2, n_o + 1)),
            dma((n_o,)), dma((n_o,)),
            dma((n_y - 1, 2, n_o)), dma((n_y - 1, 2, n_o)),
            dma((n_o,)), dma((n_o,)),
            dma((n_dp,)), dma((n_dp,)),
            dma((n_dp,)), dma((n_dp,)),
            dma((n_vocab,)), dma((n_vocab,)),
        ],
        compiler_params=pltpu.CompilerParams(
            collective_id=0, has_side_effects=True, vmem_limit_bytes=60 * 1024 * 1024
        ),
        name="head",
    )(hidden, master, targets.reshape(1, toks), loss_mask.reshape(1, toks))
    loss_value = scal.reshape(())
    wide = feats // 8
    block = pl.BlockSpec((rows, wide), lambda j: (0, j))
    some = pl.BlockSpec((toks // 8, blk), lambda j: (j, 0))
    new_master, new_first, new_second, hidden_grad = pl.pallas_call(
        update,
        grid=(8,),
        out_shape=(jax.ShapeDtypeStruct((rows, feats), F32),) * 3 + (jax.ShapeDtypeStruct((toks, blk), BF16),),
        in_specs=[block] * 4 + [some],
        out_specs=(block,) * 3 + (some,),
        compiler_params=pltpu.CompilerParams(vmem_limit_bytes=60 * 1024 * 1024),
        name="update",
    )(clipped, master, first_moment, second_moment, hidden_grad)
    return (loss_value, hidden_grad, new_master, new_first, new_second)


def solution(mesh):
    placed = (
        P("dp", "vocab"),
        P("dp"),
        P("dp"),
        P(("vocab", "dp"), None),
        P(("vocab", "dp"), None),
        P(("vocab", "dp"), None),
    )
    return jax.shard_map(
        on_device,
        mesh=mesh,
        in_specs=placed,
        out_specs=(
            P(),
            P("dp", "vocab"),
            P(("vocab", "dp"), None),
            P(("vocab", "dp"), None),
            P(("vocab", "dp"), None),
        ),
        check_vma=False,
    )
```
